128 devices in a mesh: text: 16 (over y, x), col: 8 (over z, core).
Axes of the slice: x: 4, y: 4, z: 4, core: 2. Of those that a mesh axis runs over, the one named last changes fastest.
Arguments:
- states: bfloat16 [16384, 16, 2048], P(('text', 'col')), may hold values from -6 to 6
- enc_weight: bfloat16 [2048, 1024], replicated, may hold values from -0.125 to 0.125
- self_weight: bfloat16 [1024, 1024], replicated, may hold values from -0.1875 to 0.1875
- neighbour_weight: bfloat16 [1024, 1024], replicated, may hold values from -0.1875 to 0.1875
- edge_weight: bfloat16 [16384, 8, 16, 128], P('text', 'col'), may hold values from 0.099609375 to 1
- tile_live: int32 [128, 8, 16], P('text', 'col'), may hold values from 0 to 1, as said below
- out_grad: bfloat16 [16384, 1024], P(('text', 'col')), may hold values from -6 to 6
- overflow: int32 [1], replicated, may hold values from 0 to 1024
Outputs:
- node_out: bfloat16 [16384, 1024], P(('text', 'col'))
- enc_grad: float32 [2048, 1024], P(('text', 'col'))
The draws below stay inside these ranges and needn't reach their ends.
Inputs may be any that keep to these rules, and one draw needn't show every extreme that they name: `tile_live`: 0 or 1 for each tile. No bound on how many tiles are live, in all or in any row block, may be relied on.
All inputs are finite; a program needn't handle non-finite values.
Results may differ from the reference program's by a relative error of at most 0.006.
Values may be sent and summed in bfloat16 or wider, within the bound.
A program may use at most 128 MiB of HBM per device.

```python
import math
import jax
import jax.numpy as jnp
from jax import lax

D = 2048
H = 1024
SEQ = 16
BLK = 128
TILE = 128
NODES = 16384
N_TEXT = 16
N_COL = 8


def draw_tile_live(key, part):
    key = jax.random.fold_in(key, 7)
    rate_key, cell_key = jax.random.split(key)
    row_tiles = NODES // TILE
    shard_rows = row_tiles // N_TEXT
    levels = jax.random.randint(rate_key, (N_TEXT,), 4, 17)
    row_level = jnp.repeat(levels, shard_rows)
    cells = jax.random.randint(cell_key, (row_tiles, N_COL, N_TEXT), 0, 128)
    live = (cells < row_level[:, None, None]).astype(jnp.int32)
    live = live.at[0, 0, 0].set(1)
    live = live.at[row_tiles - 1, N_COL - 1, N_TEXT - 1].set(0)
    return live


def block_levels(key, extent, cuts, smallest, largest):
    def one(position, parts):
        steps = jax.random.uniform(jax.random.fold_in(jax.random.fold_in(key, 6), position), (parts,), jnp.float32, smallest / len(cuts), largest / len(cuts))
        return jnp.repeat(jnp.exp(steps), extent[position] // parts).reshape((-1,) + (1,) * (len(extent) - position - 1))

    loudness = one(*cuts[0])
    for cut in cuts[1:]:
        loudness = loudness * one(*cut)
    return loudness


def gaussian(key, shape, scale, reach, pieces=(), held_as=jnp.bfloat16):
    gain = block_levels(key, shape, pieces, -0.22, 0.18) if pieces else 1.0
    entries = jax.random.normal(key, shape, jnp.float32) * scale * gain
    return jnp.minimum(jnp.maximum(entries, -reach), reach).astype(held_as)


def setup_inputs(seed: int = 0) -> dict:
    keys = jax.random.split(jax.random.key(seed), 9)
    return {
        "states": gaussian(keys[0], (NODES, SEQ, D), 1.0, 6.0, ((0, 128),)),
        "enc_weight": gaussian(keys[1], (D, H), D ** -0.5, 0.125),
        "self_weight": gaussian(keys[2], (H, H), H ** -0.5, 0.1875),
        "neighbour_weight": gaussian(keys[3], (H, H), H ** -0.5, 0.1875),
        "edge_weight": jnp.clip(0.099609375 + 0.9003906 * jax.random.uniform(keys[4], (NODES, N_COL, N_TEXT, BLK), jnp.float32) ** block_levels(keys[4], (NODES, N_COL, N_TEXT, BLK), ((0, 16), (1, 8)), -0.2, 0.2), 0.099609375, 1.0).astype(jnp.bfloat16),
        "tile_live": draw_tile_live(jax.random.fold_in(keys[8], 71), 0),
        "out_grad": gaussian(keys[6], (NODES, H), 1.0, 6.0, ((0, 128),)),
        "overflow": jax.random.randint(keys[7], (1,), 0, 1025).astype(jnp.int32),
    }


def encode(block, enc_weight):
    zeta = jnp.dot(block.reshape(-1, D), enc_weight, preferred_element_type=jnp.float32)
    return zeta.reshape(-1, SEQ, H)

def reference(states, enc_weight, self_weight, neighbour_weight, edge_weight, tile_live, out_grad, overflow):
    blocks = states.reshape(NODES // BLK, BLK, SEQ, D)
    input_features = lax.map(lambda b: lax.optimization_barrier(jnp.mean(jnp.tanh(encode(b, enc_weight)), axis=1)), blocks)
    input_features = input_features.reshape(NODES, H).astype(jnp.bfloat16)
    live = jnp.repeat(tile_live, TILE, axis=0)[:, :, :, None].astype(jnp.bfloat16)
    masked = edge_weight * live
    neighbour_matrix = jnp.transpose(masked, (0, 2, 1, 3)).reshape(NODES, NODES)
    node_degree = lax.optimization_barrier(jnp.sum(neighbour_matrix, axis=1, dtype=jnp.float32))
    inverse_root_degree = lax.rsqrt(1.0 + node_degree)
    pooled_neighbours = (jnp.dot(neighbour_matrix, input_features, preferred_element_type=jnp.float32) * inverse_root_degree[:, None]).astype(jnp.bfloat16)
    pre = jnp.dot(input_features, self_weight, preferred_element_type=jnp.float32) + jnp.dot(pooled_neighbours, neighbour_weight, preferred_element_type=jnp.float32)
    node_out = jax.nn.silu(pre).astype(jnp.bfloat16)
    sig = jax.nn.sigmoid(pre)
    preactivation_gradient = (out_grad.astype(jnp.float32) * sig * (1.0 + pre * (1.0 - sig))).astype(jnp.bfloat16)
    dself = jnp.dot(preactivation_gradient, self_weight.T, preferred_element_type=jnp.float32)
    pooled_gradient = (jnp.dot(preactivation_gradient, neighbour_weight.T, preferred_element_type=jnp.float32) * inverse_root_degree[:, None]).astype(jnp.bfloat16)
    dneigh = jnp.dot(neighbour_matrix.T, pooled_gradient, preferred_element_type=jnp.float32)
    dx0 = (dself + dneigh).reshape(NODES // BLK, BLK, H)

    def accumulate(total, pair):
        block, grad_block = pair
        squash = jnp.tanh(encode(block, enc_weight))
        dzeta = (grad_block[:, None, :] / SEQ * (1.0 - squash * squash)).astype(jnp.bfloat16)
        term = jnp.dot(block.reshape(-1, D).T, dzeta.reshape(-1, H), preferred_element_type=jnp.float32)
        return (total + term, 0)
    raw, _ = lax.scan(accumulate, jnp.zeros((D, H), jnp.float32), (blocks, dx0))
    factor = 1024.0 / (1024.0 + overflow[0].astype(jnp.float32))
    enc_grad = raw * factor * (SEQ / math.sqrt(NODES * SEQ))
    return (node_out, enc_grad)
```

```python
import math

import jax
import jax.numpy as jnp
from jax import lax
from jax.experimental import pallas as pl
from jax.experimental.pallas import tpu as pltpu
from jax.sharding import PartitionSpec as P

MESH = pl.DeviceIdType.MESH
BF = jnp.bfloat16
F32 = jnp.float32
NC = 4
W = 256
STEPS = (1, 2, 3)


def dot(a, b):
    return jnp.dot(a, b, preferred_element_type=F32)


def dot_nt(a, b):
    return lax.dot_general(a, b, (((1,), (1,)), ((), ())), preferred_element_type=F32)


def kernel(
    states_h, enc_h, self_h, neigh_h, edge_h, grad_h, live, overflow,
    node_out, enc_grad,
    states, enc, w_self, w_neigh, edge, edge_f, adj, squash, feats, part, out_grad,
    core_out, core_in, zed_out, zed_in, deg_out, deg_in,
    pre, dagg, dself, hop1_in, keep, hop2_in, dzeta, rcore_in, rzed_in, rx_in, ry_in,
    sums, last,
    load_sem, ag_s, ag_r, deg_s, deg_r, core_s, core_r, zed_s, zed_r, dg_s, dg_r, fw_s, fw_r,
    h1_s, h1_r, h2_s, h2_r, rc_s, rc_r, rz_s, rz_r, rx_s, rx_r, ry_s, ry_r,
):
    t = lax.axis_index("text")
    c = lax.axis_index("col")
    y, x, z, k = t // 4, t % 4, c // 2, c % 2
    other = 1 - k

    def at_x(d):
        return (y * 4 + (x + d) % 4, c)

    def at_y(d):
        return (((y + d) % 4) * 4 + x, c)

    def at_z(d):
        return (t, ((z + d) % 4) * 2 + k)

    def at_col(d):
        return (t, (c + d) % 8)

    sibling = (t, z * 2 + other)

    def send(src, dst, ssem, rsem, to):
        copy = pltpu.make_async_remote_copy(
            src_ref=src, dst_ref=dst, send_sem=ssem, recv_sem=rsem, device_id=to,
            device_id_type=MESH,
        )
        copy.start()
        return copy

    def load_states(m):
        rows = pl.ds(m * 256, 256)
        return pltpu.make_async_copy(states_h.at[rows], states.at[rows], load_sem.at[m])

    def load_enc(j):
        return pltpu.make_async_copy(enc_h.at[:, pl.ds(j * W, W)], enc.at[j], load_sem.at[8 + j])

    load_enc(0).start()
    for m in range(8):
        load_states(m).start()
    for j in range(1, NC):
        load_enc(j).start()
    rest = [
        pltpu.make_async_copy(src, dst, load_sem.at[12 + n])
        for n, (src, dst) in enumerate(
            [(edge_h, edge), (self_h, w_self), (neigh_h, w_neigh), (grad_h, out_grad)]
        )
    ]
    for copy in rest:
        copy.start()

    barrier = pltpu.get_barrier_semaphore()
    for d in STEPS:
        pl.semaphore_signal(barrier, inc=1, device_id=at_x(d), device_id_type=MESH)
        pl.semaphore_signal(barrier, inc=1, device_id=at_y(d), device_id_type=MESH)
    for d in range(1, 8):
        pl.semaphore_signal(barrier, inc=1, device_id=at_col(d), device_id_type=MESH)

    def encode(j):
        load_enc(j).wait()

        def tile(m, _):
            rows = pl.ds(m * 256, 256)
            if j == 0:
                load_states(m).wait()
            s = jnp.tanh(dot(states[rows, :], enc[j]))
            squash[j, rows, :] = s
            mean = jnp.sum(s.reshape(16, 16, W), axis=1) * (1.0 / 16.0)
            feats[j, y, x, pl.ds(m * 16, 16), :] = mean.astype(BF)
            return 0

        lax.fori_loop(0, 8, tile, 0)

    LO, HI = pl.ds(0, 64), pl.ds(64, 64)

    def gather1(j):
        own_a, own_b = feats.at[j, y, x, LO], feats.at[j, y, x, HI]
        return [
            send(own_a, own_a, ag_s.at[j, d - 1], ag_r.at[j, d - 1], at_x(d)) for d in STEPS
        ] + [
            send(own_b, own_b, ag_s.at[j, 2 + d], ag_r.at[j, 2 + d], at_y(d)) for d in STEPS
        ]

    def gather2(j, first):
        for copy in first[:3]:
            copy.wait_recv()
        row = feats.at[j, y, :, LO]
        out = [
            send(row, row, ag_s.at[j, 5 + d], ag_r.at[j, 5 + d], at_y(d)) for d in STEPS
        ]
        for copy in first[3:]:
            copy.wait_recv()
        column = feats.at[j, :, x, HI]
        return out + [
            send(column, column, ag_s.at[j, 8 + d], ag_r.at[j, 8 + d], at_x(d)) for d in STEPS
        ]

    def adjacency(r, _):
        rows = pl.ds(r * 128, 128)
        edge_f[...] = edge[rows].astype(F32).reshape(2048, 128)
        total = jnp.zeros((128, 128), F32)
        for i in range(16):
            a = edge_f[pl.ds(i, 128, stride=16), :] * live[r, i].astype(F32)
            adj[rows, i * 128 : (i + 1) * 128] = a.astype(BF)
            total = total + a
        column = jnp.broadcast_to(jnp.sum(total, axis=1, keepdims=True), (128, 128))
        deg_out[r] = column.T[0:8, :]
        return 0

    def aggregate(j, second):
        for copy in second:
            copy.wait_recv()
        slot = j % 2
        chunk = feats[j].reshape(2048, W)

        def tile(q, _):
            rows = pl.ds(q * 256, 256)
            part[slot, q] = dot(adj[rows, :], chunk).reshape(2, 128, W)
            core_out[j, q] = part[slot, q, other].astype(BF)
            return 0

        lax.fori_loop(0, 4, tile, 0)
        return send(core_out.at[j], core_in.at[j], core_s.at[j], core_r.at[j], sibling)

    def column_sum(j, copy):
        copy.wait_recv()
        for q in range(4):
            part[j % 2, q, k] = part[j % 2, q, k] + core_in[j, q].astype(F32)
            zed_out[j, q] = part[j % 2, q, k].astype(BF)
        return [
            send(
                zed_out.at[j, (z + d) % 4], zed_in.at[j, d - 1],
                zed_s.at[j, d - 1], zed_r.at[j, d - 1], at_z(d),
            )
            for d in STEPS
        ]

    def combine(j, copies, scale):
        for copy in copies:
            copy.wait_recv()
        total = part[j % 2, z, k]
        for d in range(3):
            total = total + zed_in[j, d].astype(F32)
        pooled = (total * scale).astype(BF)
        rows = pl.ds(j * W, W)
        term = dot(feats[j, y, x], w_self[rows, :]) + dot(pooled, w_neigh[rows, :])
        pre[...] = term if j == 0 else pre[...] + term

    sends = []
    encode(0)
    pl.semaphore_wait(barrier, 13)
    first, second = [gather1(0)], []
    for j in range(1, NC):
        encode(j)
        first.append(gather1(j))
        second.append(gather2(j - 1, first[j - 1]))
    rest[0].wait()
    second.append(gather2(NC - 1, first[NC - 1]))
    lax.fori_loop(0, 8, adjacency, 0)
    deg_copies = [
        send(
            deg_out.at[(c + d) % 8], deg_in.at[d - 1], deg_s.at[d - 1], deg_r.at[d - 1], at_col(d)
        )
        for d in range(1, 8)
    ]

    def flip(m, _):
        def pair(n, _):
            a, b = pl.ds(m * 256, 256), pl.ds(n * 256, 256)
            up, down = states[a, b], states[b, a]
            states[a, b] = down.T
            states[b, a] = up.T
            return 0

        lax.fori_loop(0, m + 1, pair, 0)
        return 0

    lax.fori_loop(0, 8, flip, 0)

    for copy in deg_copies:
        copy.wait_recv()
    degree = deg_out[c]
    for d in range(7):
        degree = degree + deg_in[d]
    inv_row = lax.rsqrt(1.0 + degree)[0:1, :]
    inv_column = jnp.broadcast_to(inv_row, (128, 128)).T[:, 0:1]

    for copy in rest[1:]:
        copy.wait()
    core, zed = [], []
    for j in range(NC):
        core.append(aggregate(j, second[j]))
        zed.append(column_sum(j, core[j]))
        if j >= 1:
            combine(j - 1, zed[j - 1], inv_column)
    combine(NC - 1, zed[NC - 1], inv_column)

    v = pre[...]
    sg = 1.0 / (1.0 + jnp.exp(-v))
    node_out[...] = (v * sg).astype(BF)
    dpre = (out_grad[...].astype(F32) * sg * (1.0 + v * (1.0 - sg))).astype(BF)

    around = []
    for j in range(NC):
        rows = pl.ds(j * W, W)
        dagg[j, c] = (dot_nt(w_neigh[rows, :], dpre) * inv_row).astype(BF)
        own = dagg.at[j, c]
        around.append(
            [send(own, own, dg_s.at[j, d - 1], dg_r.at[j, d - 1], at_z(d)) for d in STEPS]
            + [send(own, own, dg_s.at[j, 3], dg_r.at[j, 3], sibling)]
        )
    for j in range(NC):
        dself[j] = dot_nt(w_self[pl.ds(j * W, W), :], dpre)

    for copies in first + second + zed:
        for copy in copies:
            copy.wait_send()
    for copy in core + deg_copies:
        copy.wait_send()

    A, B = pl.ds(0, 128), pl.ds(128, 128)

    def forward(j):
        out = []
        for d in STEPS:
            around[j][d - 1].wait_recv()
            block = dagg.at[j, ((z - d + 4) % 4) * 2 + k]
            out.append(send(block, block, fw_s.at[j, d - 1], fw_r.at[j, d - 1], sibling))
        return out

    def scatter1(j, passed):
        around[j][3].wait_recv()
        for copy in passed:
            copy.wait_recv()
        chunk = jnp.concatenate([dagg[j, q] for q in range(8)], axis=1)

        def tile(n, _):
            p = dot(chunk, adj[:, pl.ds(pl.multiple_of(n * 256, 256), 256)]).astype(BF)
            for i in range(2):
                block = p[:, i * 128 : (i + 1) * 128]
                yy, xx = n // 2, (n % 2) * 2 + i
                feats[j, yy, xx, :, 0:128] = block[0:128]
                feats[j, yy, xx, :, 128:256] = block[128:256]
            return 0

        lax.fori_loop(0, 8, tile, 0)
        out = []
        for d in STEPS:
            out.append(
                send(
                    feats.at[j, (y + d) % 4, :, :, A], hop1_in.at[j, 0, d - 1],
                    h1_s.at[j, d - 1], h1_r.at[j, d - 1], at_y(d),
                )
            )
            out.append(
                send(
                    feats.at[j, :, (x + d) % 4, :, B], hop1_in.at[j, 1, d - 1],
                    h1_s.at[j, 2 + d], h1_r.at[j, 2 + d], at_x(d),
                )
            )
        return out

    def scatter2(j, copies):
        for copy in copies:
            copy.wait_recv()
        for q in range(4):
            a = feats[j, y, q, :, 0:128].astype(F32)
            b = feats[j, q, x, :, 128:256].astype(F32)
            for d in range(3):
                a = a + hop1_in[j, 0, d, q].astype(F32)
                b = b + hop1_in[j, 1, d, q].astype(F32)
            part[0, q, 0, :, 0:128] = a
            part[0, q, 0, :, 128:256] = b
            core_out[j, q, :, 0:128] = a.astype(BF)
            core_out[j, q, :, 128:256] = b.astype(BF)
        keep[j, 0] = part[0, x, 0, :, 0:128]
        keep[j, 1] = part[0, y, 0, :, 128:256]
        out = []
        for d in STEPS:
            out.append(
                send(
                    core_out.at[j, (x + d) % 4, :, A], hop2_in.at[j, 0, d - 1],
                    h2_s.at[j, d - 1], h2_r.at[j, d - 1], at_x(d),
                )
            )
            out.append(
                send(
                    core_out.at[j, (y + d) % 4, :, B], hop2_in.at[j, 1, d - 1],
                    h2_s.at[j, 2 + d], h2_r.at[j, 2 + d], at_y(d),
                )
            )
        return out

    def encoder_term(j, copies):
        for copy in copies:
            copy.wait_recv()
        halves = []
        for h in range(2):
            total = keep[j, h]
            for d in range(3):
                total = total + hop2_in[j, h, d].astype(F32)
            halves.append(total)
        dx0 = jnp.concatenate(halves, axis=0) + dself[j]
        part[1, 0, 0] = dx0.T * (1.0 / 16.0)

        def tile(m, _):
            rows = pl.ds(m * 256, 256)
            s = squash[j, rows, :].reshape(16, 16, W)
            g = part[1, 0, 0, pl.ds(m * 16, 16), :].reshape(16, 1, W)
            dzeta[rows, :] = (g * (1.0 - s * s)).astype(BF).reshape(256, W)
            return 0

        lax.fori_loop(0, 8, tile, 0)

        def term(m, _):
            rows = pl.ds(m * 256, 256)
            squash[j, rows, :] = dot(states[rows, :], dzeta[...])
            for g in range(8):
                away = squash[j, pl.ds(m * 256 + g * 32 + other * 16, 16), :].astype(BF)
                enc[j, pl.ds(m * 128 + g * 16, 16), :] = away
            return 0

        lax.fori_loop(0, 8, term, 0)
        return send(
            enc.at[j, pl.ds(0, 1024)], rcore_in.at[j], rc_s.at[j], rc_r.at[j], sibling
        )

    def term_zed(j, copy):
        copy.wait_recv()

        def tile(m, _):
            for q in range(4):
                g = m * 4 + q
                mine = pl.ds(g * 32 + k * 16, 16)
                total = squash[j, mine, :] + rcore_in[j, pl.ds(g * 16, 16), :].astype(F32)
                squash[j, mine, :] = total
                enc[j, pl.ds(1024 + q * 256 + m * 16, 16), :] = total.astype(BF)
            return 0

        lax.fori_loop(0, 16, tile, 0)
        return [
            send(
                enc.at[j, pl.ds(1024 + ((z + d) % 4) * 256, 256)], rzed_in.at[j, d - 1],
                rz_s.at[j, d - 1], rz_r.at[j, d - 1], at_z(d),
            )
            for d in STEPS
        ]

    def term_x(j, copies):
        for copy in copies:
            copy.wait_recv()

        def tile(m, _):
            total = squash[j, pl.ds((m * 4 + z) * 32 + k * 16, 16), :]
            for d in range(3):
                total = total + rzed_in[j, d, pl.ds(m * 16, 16), :].astype(F32)
            rx_out = pl.ds((m % 4) * 64 + (m // 4) * 16, 16)
            sums[j, rx_out, :] = total
            return 0

        lax.fori_loop(0, 16, tile, 0)
        return [
            send(
                sums.at[j, pl.ds(((x + d) % 4) * 64, 64)], rx_in.at[j, d - 1],
                rx_s.at[j, d - 1], rx_r.at[j, d - 1], at_x(d),
            )
            for d in STEPS
        ]

    def term_y(j, copies):
        for copy in copies:
            copy.wait_recv()
        total = sums[j, pl.ds(x * 64, 64), :]
        for d in range(3):
            total = total + rx_in[j, d]
        last[j] = total
        return [
            send(
                last.at[j, pl.ds(((y + d) % 4) * 16, 16)], ry_in.at[j, d - 1],
                ry_s.at[j, d - 1], ry_r.at[j, d - 1], at_y(d),
            )
            for d in STEPS
        ]

    factor = 1024.0 / (1024.0 + overflow[0].astype(F32)) * (16.0 / math.sqrt(16384 * 16))

    def finish(j, copies):
        for copy in copies:
            copy.wait_recv()
        total = last[j, pl.ds(y * 16, 16), :]
        for d in range(3):
            total = total + ry_in[j, d]
        enc_grad[:, j * W : (j + 1) * W] = total * factor

    passed, hop1, hop2 = [forward(0)], [], []
    for j in range(NC - 1):
        passed.append(forward(j + 1))
        hop1.append(scatter1(j, passed[j]))
    hop2.append(scatter2(0, hop1[0]))
    hop1.append(scatter1(NC - 1, passed[NC - 1]))
    rcore, rzed, rx, ry = [], [], [], []
    for j in range(NC):
        rcore.append(encoder_term(j, hop2[j]))
        if j + 1 < NC:
            hop2.append(scatter2(j + 1, hop1[j + 1]))
        if j >= 1:
            rzed.append(term_zed(j - 1, rcore[j - 1]))
        if j >= 2:
            rx.append(term_x(j - 2, rzed[j - 2]))
        if j >= 3:
            ry.append(term_y(j - 3, rx[j - 3]))
    rzed.append(term_zed(NC - 1, rcore[NC - 1]))
    rx.append(term_x(NC - 2, rzed[NC - 2]))
    ry.append(term_y(NC - 3, rx[NC - 3]))
    finish(0, ry[0])
    rx.append(term_x(NC - 1, rzed[NC - 1]))
    ry.append(term_y(NC - 2, rx[NC - 2]))
    finish(1, ry[1])
    ry.append(term_y(NC - 1, rx[NC - 1]))
    finish(2, ry[2])
    finish(3, ry[3])

    for copies in around + passed + hop1 + hop2 + rzed + rx + ry:
        for copy in copies:
            copy.wait_send()
    for copy in rcore:
        copy.wait_send()


def local(
    states, enc_weight, self_weight, neighbour_weight, edge_weight, tile_live, out_grad, overflow
):
    states = states.reshape(2048, 2048)
    edge_weight = edge_weight.reshape(1024, 16, 128)
    tile_live = tile_live.reshape(8, 16)
    hbm = pl.BlockSpec(memory_space=pl.ANY)
    smem = pl.BlockSpec(memory_space=pltpu.SMEM)
    vmem = pl.BlockSpec(memory_space=pltpu.VMEM)
    V, S = pltpu.VMEM, pltpu.SemaphoreType.DMA
    buffers = [
        V((2048, 2048), BF),
        V((NC, 2048, W), BF),
        V((1024, 1024), BF),
        V((1024, 1024), BF),
        V((1024, 16, 128), BF),
        V((2048, 128), F32),
        V((1024, 2048), BF),
        V((NC, 2048, W), F32),
        V((NC, 4, 4, 128, W), BF),
        V((2, 4, 2, 128, W), F32),
        V((128, 1024), BF),
        V((NC, 4, 128, W), BF),
        V((NC, 4, 128, W), BF),
        V((NC, 4, 128, W), BF),
        V((NC, 3, 128, W), BF),
        V((8, 8, 128), F32),
        V((7, 8, 128), F32),
        V((128, 1024), F32),
        V((NC, 8, W, 128), BF),
        V((NC, W, 128), F32),
        V((NC, 2, 3, 4, 128, 128), BF),
        V((NC, 2, 128, 128), F32),
        V((NC, 2, 3, 128, 128), BF),
        V((2048, W), BF),
        V((NC, 1024, W), BF),
        V((NC, 3, 256, W), BF),
        V((NC, 3, 64, W), F32),
        V((NC, 3, 16, W), F32),
        V((NC, 256, W), F32),
        V((NC, 64, W), F32),
    ]
    shapes = [
        (NC, 12), (7,), (NC,), (NC, 3), (NC, 4), (NC, 3), (NC, 6), (NC, 6), (NC,), (NC, 3),
        (NC, 3), (NC, 3),
    ]
    semaphores = [S((16,))] + [S(shape) for shape in shapes for _ in range(2)]
    return pl.pallas_call(
        kernel,
        out_shape=(
            jax.ShapeDtypeStruct((128, 1024), BF),
            jax.ShapeDtypeStruct((16, 1024), F32),
        ),
        in_specs=[hbm] * 6 + [smem] * 2,
        out_specs=(vmem, vmem),
        scratch_shapes=buffers + semaphores,
        compiler_params=pltpu.CompilerParams(
            collective_id=0, has_side_effects=True, vmem_limit_bytes=63 * 1024 * 1024
        ),
        name="step",
    )(states, enc_weight, self_weight, neighbour_weight, edge_weight, out_grad, tile_live, overflow)


def solution(mesh):
    in_specs = (
        P(("text", "col"), None, None),
        P(),
        P(),
        P(),
        P("text", "col", None, None),
        P("text", "col", None),
        P(("text", "col"), None),
        P(),
    )
    out_specs = (P(("text", "col"), None), P(("text", "col"), None))
    return jax.shard_map(local, mesh=mesh, in_specs=in_specs, out_specs=out_specs, check_vma=False)
```

```python
import math

import jax
import jax.numpy as jnp
from jax import lax
from jax.experimental import pallas as pl
from jax.experimental.pallas import tpu as pltpu
from jax.sharding import PartitionSpec as P

MESH = pl.DeviceIdType.MESH
BF = jnp.bfloat16
F32 = jnp.float32
NC = 4
W = 256
STEPS = (1, 2, 3)


def dot(a, b):
    return jnp.dot(a, b, preferred_element_type=F32)


def dot_nt(a, b):
    return lax.dot_general(a, b, (((1,), (1,)), ((), ())), preferred_element_type=F32)


def kernel(
    states_h, enc_h, self_h, neigh_h, edge_h, grad_h, live, overflow,
    node_out, enc_grad,
    states, enc, w_self, w_neigh, edge, edge_f, adj, squash, feats, part, out_grad,
    core_out, core_in, zed_out, zed_in, deg_out, deg_in,
    pre, dagg, dself, hop1_in, keep, hop2_in, dzeta, rcore_in, rzed_in, rx_in, ry_in,
    sums, sums_out, last,
    load_sem, ag_s, ag_r, deg_s, deg_r, core_s, core_r, zed_s, zed_r, dg_s, dg_r, fw_s, fw_r,
    h1_s, h1_r, h2_s, h2_r, rc_s, rc_r, rz_s, rz_r, rx_s, rx_r, ry_s, ry_r,
):
    t = lax.axis_index("text")
    c = lax.axis_index("col")
    y, x, z, k = t // 4, t % 4, c // 2, c % 2
    other = 1 - k

    def at_x(d):
        return (y * 4 + (x + d) % 4, c)

    def at_y(d):
        return (((y + d) % 4) * 4 + x, c)

    def at_z(d):
        return (t, ((z + d) % 4) * 2 + k)

    def at_col(d):
        return (t, (c + d) % 8)

    sibling = (t, z * 2 + other)

    def describe(src, dst, ssem, rsem, to):
        return pltpu.make_async_remote_copy(
            src_ref=src, dst_ref=dst, send_sem=ssem, recv_sem=rsem, device_id=to,
            device_id_type=MESH,
        )

    def send(src, dst, ssem, rsem, to):
        copy = describe(src, dst, ssem, rsem, to)
        copy.start()
        return copy

    def load_states(m):
        rows = pl.ds(m * 256, 256)
        return pltpu.make_async_copy(states_h.at[rows], states.at[rows], load_sem.at[m])

    def load_enc(j):
        return pltpu.make_async_copy(enc_h.at[:, pl.ds(j * W, W)], enc.at[j], load_sem.at[8 + j])

    load_enc(0).start()
    for m in range(8):
        load_states(m).start()
    for j in range(1, NC):
        load_enc(j).start()
    rest = [
        pltpu.make_async_copy(src, dst, load_sem.at[12 + n])
        for n, (src, dst) in enumerate(
            [(edge_h, edge), (self_h, w_self), (neigh_h, w_neigh), (grad_h, out_grad)]
        )
    ]
    for copy in rest:
        copy.start()

    barrier = pltpu.get_barrier_semaphore()
    for d in STEPS:
        pl.semaphore_signal(barrier, inc=1, device_id=at_x(d), device_id_type=MESH)
        pl.semaphore_signal(barrier, inc=1, device_id=at_y(d), device_id_type=MESH)
    for d in range(1, 8):
        pl.semaphore_signal(barrier, inc=1, device_id=at_col(d), device_id_type=MESH)

    def encode(j):
        load_enc(j).wait()

        size = 512 if j == 0 else 1024

        def tile(m, _):
            rows = pl.ds(m * size, size)
            if j == 0:
                load_states(2 * m).wait()
                load_states(2 * m + 1).wait()
            s = jnp.tanh(dot(states[rows, :], enc[j]))
            squash[j, rows, :] = s
            mean = jnp.sum(s.reshape(size // 16, 16, W), axis=1) * (1.0 / 16.0)
            feats[j, y, x, pl.ds(m * (size // 16), size // 16), :] = mean.astype(BF)
            return 0

        lax.fori_loop(0, 2048 // size, tile, 0)

    LO, HI = pl.ds(0, 64), pl.ds(64, 64)

    def gather1(j):
        own_a, own_b = feats.at[j, y, x, LO], feats.at[j, y, x, HI]
        return [
            send(own_a, own_a, ag_s.at[j, d - 1], ag_r.at[j, d - 1], at_x(d)) for d in STEPS
        ] + [
            send(own_b, own_b, ag_s.at[j, 2 + d], ag_r.at[j, 2 + d], at_y(d)) for d in STEPS
        ]

    def gather2(j, first):
        for copy in first[:3]:
            copy.wait_recv()
        row = feats.at[j, y, :, LO]
        out = [
            send(row, row, ag_s.at[j, 6 + n], ag_r.at[j, 6 + n], at_y(d))
            for n, d in enumerate((1, 3))
        ]
        for copy in first[3:]:
            copy.wait_recv()
        column = feats.at[j, :, x, HI]
        return out + [
            send(column, column, ag_s.at[j, 8 + n], ag_r.at[j, 8 + n], at_x(d))
            for n, d in enumerate((1, 3))
        ]

    def gather3(j, second):
        out = []
        for n, d in enumerate((1, 3)):
            half = pl.ds(2 * n, 2)
            second[n].wait_recv()
            row = feats.at[j, (y + 4 - d) % 4, half, LO]
            out.append(send(row, row, ag_s.at[j, 10 + n], ag_r.at[j, 10 + n], at_y(d)))
            second[2 + n].wait_recv()
            column = feats.at[j, half, (x + 4 - d) % 4, HI]
            out.append(send(column, column, ag_s.at[j, 12 + n], ag_r.at[j, 12 + n], at_x(d)))
        return out

    def adjacency(r, _):
        rows = pl.ds(r * 128, 128)
        edge_f[...] = edge[rows].astype(F32).reshape(2048, 128)
        total = jnp.zeros((128, 128), F32)
        for i in range(16):
            a = edge_f[pl.ds(i, 128, stride=16), :] * live[r, i].astype(F32)
            adj[rows, i * 128 : (i + 1) * 128] = a.astype(BF)
            total = total + a
        column = jnp.broadcast_to(jnp.sum(total, axis=1, keepdims=True), (128, 128))
        deg_out[r] = column.T[0:8, :]
        return 0

    def aggregate(j, third):
        for copy in third:
            copy.wait_recv()
        p = dot(adj[...], feats[j].reshape(2048, W)).reshape(4, 2, 128, W)
        part[j] = jnp.where(k == 0, p[:, 0], p[:, 1])
        core_out[j] = jnp.where(k == 0, p[:, 1], p[:, 0]).astype(BF)
        return send(core_out.at[j], core_in.at[j], core_s.at[j], core_r.at[j], sibling)

    def column_sum(j, copy):
        copy.wait_recv()
        for q in range(4):
            part[j, q] = part[j, q] + core_in[j, q].astype(F32)
            zed_out[j, q] = part[j, q].astype(BF)
        return [
            send(
                zed_out.at[j, (z + d) % 4], zed_in.at[j, d - 1],
                zed_s.at[j, d - 1], zed_r.at[j, d - 1], at_z(d),
            )
            for d in STEPS
        ]

    def combine(j, copies, scale):
        for copy in copies:
            copy.wait_recv()
        total = part[j, z]
        for d in range(3):
            total = total + zed_in[j, d].astype(F32)
        pooled = (total * scale).astype(BF)
        pre[...] += dot(pooled, w_neigh[pl.ds(j * W, W), :])

    encode(0)
    pl.semaphore_wait(barrier, 13)
    first, second, third = [gather1(0)], [], []
    for j in range(1, NC):
        encode(j)
        first.append(gather1(j))
        second.append(gather2(j - 1, first[j - 1]))
    third.append(gather3(0, second[0]))
    rest[0].wait()
    lax.fori_loop(0, 4, adjacency, 0)
    second.append(gather2(NC - 1, first[NC - 1]))
    third.append(gather3(1, second[1]))
    lax.fori_loop(4, 8, adjacency, 0)
    deg_copies = [
        send(
            deg_out.at[(c + d) % 8], deg_in.at[d - 1], deg_s.at[d - 1], deg_r.at[d - 1], at_col(d)
        )
        for d in range(1, 8)
    ]
    third.append(gather3(2, second[2]))
    core, zed = [aggregate(0, third[0])], []

    def flip(m, _):
        def pair(n, _):
            a, b = pl.ds(m * 256, 256), pl.ds(n * 256, 256)
            up, down = states[a, b], states[b, a]
            states[a, b] = down.T
            states[b, a] = up.T
            return 0

        lax.fori_loop(0, m + 1, pair, 0)
        return 0

    lax.fori_loop(0, 6, flip, 0)
    zed.append(column_sum(0, core[0]))
    core.append(aggregate(1, third[1]))
    third.append(gather3(3, second[3]))
    zed.append(column_sum(1, core[1]))
    for copy in rest[1:]:
        copy.wait()
    own = jnp.concatenate([feats[j, y, x] for j in range(NC)], axis=1)
    pre[...] = dot(own, w_self[...])
    for copy in deg_copies:
        copy.wait_recv()
    degree = deg_out[c]
    for d in range(7):
        degree = degree + deg_in[d]
    inv_row = lax.rsqrt(1.0 + degree)[0:1, :]
    inv_column = jnp.broadcast_to(inv_row, (128, 128)).T[:, 0:1]
    combine(0, zed[0], inv_column)
    core.append(aggregate(2, third[2]))
    lax.fori_loop(6, 8, flip, 0)
    zed.append(column_sum(2, core[2]))
    combine(1, zed[1], inv_column)
    core.append(aggregate(3, third[3]))
    combine(2, zed[2], inv_column)
    zed.append(column_sum(3, core[3]))
    combine(3, zed[3], inv_column)

    v = pre[...]
    sg = 1.0 / (1.0 + jnp.exp(-v))
    node_out[...] = (v * sg).astype(BF)
    dpre = (out_grad[...].astype(F32) * sg * (1.0 + v * (1.0 - sg))).astype(BF)

    around = []

    def spread(j):
        dagg[j, c] = (dot_nt(w_neigh[pl.ds(j * W, W), :], dpre) * inv_row).astype(BF)
        own = dagg.at[j, c]
        around.append(
            [send(own, own, dg_s.at[j, d - 1], dg_r.at[j, d - 1], at_z(d)) for d in STEPS]
            + [send(own, own, dg_s.at[j, 3], dg_r.at[j, 3], sibling)]
        )

    spread(0)
    spread(1)
    for j in range(NC):
        dself[j] = dot_nt(w_self[pl.ds(j * W, W), :], dpre)

    for copies in first + second + third + zed:
        for copy in copies:
            copy.wait_send()
    for copy in core + deg_copies:
        copy.wait_send()

    A, B = pl.ds(0, 128), pl.ds(128, 128)

    def forward(j):
        out = []
        for d in STEPS:
            around[j][d - 1].wait_recv()
            block = dagg.at[j, ((z - d + 4) % 4) * 2 + k]
            out.append(send(block, block, fw_s.at[j, d - 1], fw_r.at[j, d - 1], sibling))
        return out

    def transpose_product(j, passed):
        around[j][3].wait_recv()
        for copy in passed:
            copy.wait_recv()
        chunk = jnp.concatenate([dagg[j, q] for q in range(8)], axis=1)
        p = dot(chunk, adj[...]).astype(BF)
        for i in range(16):
            feats[j, i // 4, i % 4, :, 0:128] = p[0:128, i * 128 : (i + 1) * 128]
            feats[j, i // 4, i % 4, :, 128:256] = p[128:256, i * 128 : (i + 1) * 128]

    LOWER, UPPER = pl.ds(0, 2), pl.ds(2, 2)
    WAYS = ((1, LOWER, UPPER), (3, UPPER, LOWER))

    def scatter1(j):
        relayed, direct = [], []
        for n, (d, via, straight) in enumerate(WAYS):
            far = (y + 2) % 4, (x + 2) % 4
            near = (y + d) % 4, (x + d) % 4
            a, b = feats.at[j, far[0], via, :, A], feats.at[j, via, far[1], :, B]
            into = pl.ds(2 * n, 2)
            relayed.append(
                send(a, hop1_in.at[j, 0, 2, into], h1_s.at[j, n], h1_r.at[j, n], at_y(d))
            )
            relayed.append(
                send(b, hop1_in.at[j, 1, 2, into], h1_s.at[j, 2 + n], h1_r.at[j, 2 + n], at_x(d))
            )
            a, b = feats.at[j, near[0], straight, :, A], feats.at[j, straight, near[1], :, B]
            direct.append(
                send(a, hop1_in.at[j, 0, n, straight], h1_s.at[j, 4 + n], h1_r.at[j, 4 + n], at_y(d))
            )
            direct.append(
                send(b, hop1_in.at[j, 1, n, straight], h1_s.at[j, 6 + n], h1_r.at[j, 6 + n], at_x(d))
            )
        return relayed, direct

    def relay(j, relayed):
        out = []
        for n, (d, via, _) in enumerate(WAYS):
            relayed[2 * n].wait_recv()
            relayed[2 * n + 1].wait_recv()
            near_y, near_x = (y + d) % 4, (x + d) % 4
            for q in range(2):
                i = 2 * n + q
                a = feats[j, near_y, i, :, 0:128].astype(F32) + hop1_in[j, 0, 2, i].astype(F32)
                b = feats[j, i, near_x, :, 128:256].astype(F32) + hop1_in[j, 1, 2, i].astype(F32)
                feats[j, near_y, i, :, 0:128] = a.astype(BF)
                feats[j, i, near_x, :, 128:256] = b.astype(BF)
            a, b = feats.at[j, near_y, via, :, A], feats.at[j, via, near_x, :, B]
            out.append(
                send(a, hop1_in.at[j, 0, n, via], h1_s.at[j, 8 + n], h1_r.at[j, 8 + n], at_y(d))
            )
            out.append(
                send(b, hop1_in.at[j, 1, n, via], h1_s.at[j, 10 + n], h1_r.at[j, 10 + n], at_x(d))
            )
        return out

    def scatter2(j, copies):
        for copy in copies:
            copy.wait_recv()
        for q in range(4):
            a = feats[j, y, q, :, 0:128].astype(F32)
            b = feats[j, q, x, :, 128:256].astype(F32)
            for n in range(2):
                a = a + hop1_in[j, 0, n, q].astype(F32)
                b = b + hop1_in[j, 1, n, q].astype(F32)
            part[0, q, :, 0:128] = a
            part[0, q, :, 128:256] = b
            core_out[j, q, :, 0:128] = a.astype(BF)
            core_out[j, q, :, 128:256] = b.astype(BF)
        keep[j, 0] = part[0, x, :, 0:128]
        keep[j, 1] = part[0, y, :, 128:256]
        out = []
        for d in STEPS:
            out.append(
                send(
                    core_out.at[j, (x + d) % 4, :, A], hop2_in.at[j, 0, d - 1],
                    h2_s.at[j, d - 1], h2_r.at[j, d - 1], at_x(d),
                )
            )
            out.append(
                send(
                    core_out.at[j, (y + d) % 4, :, B], hop2_in.at[j, 1, d - 1],
                    h2_s.at[j, 2 + d], h2_r.at[j, 2 + d], at_y(d),
                )
            )
        return out

    def encoder_term(j, copies):
        for copy in copies:
            copy.wait_recv()
        halves = []
        for h in range(2):
            total = keep[j, h]
            for d in range(3):
                total = total + hop2_in[j, h, d].astype(F32)
            halves.append(total)
        dx0 = jnp.concatenate(halves, axis=0) + dself[j]
        part[1, 0] = dx0.T * (1.0 / 16.0)

        def tile(m, _):
            rows = pl.ds(m * 256, 256)
            s = squash[j, rows, :].reshape(16, 16, W)
            g = part[1, 0, pl.ds(m * 16, 16), :].reshape(16, 1, W)
            dzeta[rows, :] = (g * (1.0 - s * s)).astype(BF).reshape(256, W)
            return 0

        lax.fori_loop(0, 8, tile, 0)

        def term(m, _):
            rows = pl.ds(m * 1024, 1024)
            squash[j, rows, :] = dot(states[rows, :], dzeta[...])
            for g in range(32):
                away = squash[j, pl.ds(m * 1024 + g * 32 + other * 16, 16), :].astype(BF)
                enc[j, pl.ds(m * 512 + g * 16, 16), :] = away
            raw_half(j, m).start()
            return 0

        lax.fori_loop(0, 2, term, 0)

    def raw_half(j, m):
        rows = pl.ds(m * 512, 512)
        return describe(
            enc.at[j, rows], rcore_in.at[j, rows], rc_s.at[j, m], rc_r.at[j, m], sibling
        )

    def term_zed(j, half):
        raw_half(j, half).wait_recv()

        def tile(m, _):
            for q in range(4):
                g = m * 4 + q
                mine = pl.ds(g * 32 + k * 16, 16)
                total = squash[j, mine, :] + rcore_in[j, pl.ds(g * 16, 16), :].astype(F32)
                squash[j, mine, :] = total
                enc[j, pl.ds(1024 + q * 256 + m * 16, 16), :] = total.astype(BF)
            return 0

        lax.fori_loop(half * 8, half * 8 + 8, tile, 0)
        into = pl.ds(half * 128, 128)
        return [
            send(
                enc.at[j, pl.ds(1024 + ((z + d) % 4) * 256 + half * 128, 128)],
                rzed_in.at[j, d - 1, into],
                rz_s.at[j, half * 3 + d - 1], rz_r.at[j, half * 3 + d - 1], at_z(d),
            )
            for d in STEPS
        ]

    def term_x(j, copies):
        for copy in copies:
            copy.wait_recv()

        def tile(m, _):
            total = squash[j, pl.ds((m * 4 + z) * 32 + k * 16, 16), :]
            for d in range(3):
                total = total + rzed_in[j, d, pl.ds(m * 16, 16), :].astype(F32)
            rx_out = pl.ds((m % 4) * 64 + (m // 4) * 16, 16)
            sums[j, rx_out, :] = total
            sums_out[j, rx_out, :] = total.astype(BF)
            return 0

        lax.fori_loop(0, 16, tile, 0)
        return [
            send(
                sums_out.at[j, pl.ds(((x + d) % 4) * 64, 64)], rx_in.at[j, d - 1],
                rx_s.at[j, d - 1], rx_r.at[j, d - 1], at_x(d),
            )
            for d in STEPS
        ]

    def term_y(j, copies):
        for copy in copies:
            copy.wait_recv()
        total = sums[j, pl.ds(x * 64, 64), :]
        for d in range(3):
            total = total + rx_in[j, d].astype(F32)
        last[j] = total
        return [
            send(
                last.at[j, pl.ds(((y + d) % 4) * 16, 16)], ry_in.at[j, d - 1],
                ry_s.at[j, d - 1], ry_r.at[j, d - 1], at_y(d),
            )
            for d in STEPS
        ]

    factor = 1024.0 / (1024.0 + overflow[0].astype(F32)) * (16.0 / math.sqrt(16384 * 16))

    def finish(j, copies):
        for copy in copies:
            copy.wait_recv()
        total = last[j, pl.ds(y * 16, 16), :]
        for d in range(3):
            total = total + ry_in[j, d]
        enc_grad[:, j * W : (j + 1) * W] = total * factor

    passed, relayed, direct, hop1 = [], [], [], []
    hop2, rzed, rx, ry = [], [], [], []

    def product(j):
        passed.append(forward(j))
        if j + 2 < NC:
            spread(j + 2)
        transpose_product(j, passed[j])

    def first_hop(j):
        for kept, copies in zip((relayed, direct), scatter1(j)):
            kept.append(copies)

    def pass_on(j):
        hop1.append(relay(j, relayed[j]))

    def second_hop(j):
        hop2.append(scatter2(j, direct[j] + hop1[j]))

    def raw(j):
        encoder_term(j, hop2[j])

    def raw_z(j):
        rzed.append(term_zed(j, 0) + term_zed(j, 1))

    def raw_x(j):
        rx.append(term_x(j, rzed[j]))

    def raw_y(j):
        ry.append(term_y(j, rx[j]))

    for step, j in (
        (product, 0), (first_hop, 0), (product, 1), (pass_on, 0), (first_hop, 1), (product, 2),
        (second_hop, 0), (pass_on, 1), (first_hop, 2), (raw, 0), (second_hop, 1), (pass_on, 2),
        (product, 3), (first_hop, 3), (raw_z, 0), (raw, 1), (second_hop, 2), (pass_on, 3),
        (raw_z, 1), (raw_x, 0), (raw, 2), (second_hop, 3), (raw_z, 2), (raw_y, 0), (raw_x, 1),
        (raw, 3), (raw_y, 1), (raw_x, 2), (raw_z, 3), (raw_y, 2), (raw_x, 3), (raw_y, 3),
    ):
        step(j)
    for j in range(NC):
        finish(j, ry[j])

    for copies in around + passed + relayed + direct + hop1 + hop2 + rzed + rx + ry:
        for copy in copies:
            copy.wait_send()
    for j in range(NC):
        for half in range(2):
            raw_half(j, half).wait_send()


def local(
    states, enc_weight, self_weight, neighbour_weight, edge_weight, tile_live, out_grad, overflow
):
    states = states.reshape(2048, 2048)
    edge_weight = edge_weight.reshape(1024, 16, 128)
    tile_live = tile_live.reshape(8, 16)
    hbm = pl.BlockSpec(memory_space=pl.ANY)
    smem = pl.BlockSpec(memory_space=pltpu.SMEM)
    vmem = pl.BlockSpec(memory_space=pltpu.VMEM)
    V, S = pltpu.VMEM, pltpu.SemaphoreType.DMA
    buffers = [
        V((2048, 2048), BF),
        V((NC, 2048, W), BF),
        V((1024, 1024), BF),
        V((1024, 1024), BF),
        V((1024, 16, 128), BF),
        V((2048, 128), F32),
        V((1024, 2048), BF),
        V((NC, 2048, W), F32),
        V((NC, 4, 4, 128, W), BF),
        V((NC, 4, 128, W), F32),
        V((128, 1024), BF),
        V((NC, 4, 128, W), BF),
        V((NC, 4, 128, W), BF),
        V((NC, 4, 128, W), BF),
        V((NC, 3, 128, W), BF),
        V((8, 8, 128), F32),
        V((7, 8, 128), F32),
        V((128, 1024), F32),
        V((NC, 8, W, 128), BF),
        V((NC, W, 128), F32),
        V((NC, 2, 3, 4, 128, 128), BF),
        V((NC, 2, 128, 128), F32),
        V((NC, 2, 3, 128, 128), BF),
        V((2048, W), BF),
        V((NC, 1024, W), BF),
        V((NC, 3, 256, W), BF),
        V((NC, 3, 64, W), BF),
        V((NC, 3, 16, W), F32),
        V((NC, 256, W), F32),
        V((NC, 256, W), BF),
        V((NC, 64, W), F32),
    ]
    shapes = [
        (NC, 14), (7,), (NC,), (NC, 3), (NC, 4), (NC, 3), (NC, 12), (NC, 6), (NC, 2), (NC, 6),
        (NC, 3), (NC, 3),
    ]
    semaphores = [S((16,))] + [S(shape) for shape in shapes for _ in range(2)]
    return pl.pallas_call(
        kernel,
        out_shape=(
            jax.ShapeDtypeStruct((128, 1024), BF),
            jax.ShapeDtypeStruct((16, 1024), F32),
        ),
        in_specs=[hbm] * 6 + [smem] * 2,
        out_specs=(vmem, vmem),
        scratch_shapes=buffers + semaphores,
        compiler_params=pltpu.CompilerParams(
            collective_id=0, has_side_effects=True, vmem_limit_bytes=63 * 1024 * 1024
        ),
        name="step",
    )(states, enc_weight, self_weight, neighbour_weight, edge_weight, out_grad, tile_live, overflow)


def solution(mesh):
    in_specs = (
        P(("text", "col"), None, None),
        P(),
        P(),
        P(),
        P("text", "col", None, None),
        P("text", "col", None),
        P(("text", "col"), None),
        P(),
    )
    out_specs = (P(("text", "col"), None), P(("text", "col"), None))
    return jax.shard_map(local, mesh=mesh, in_specs=in_specs, out_specs=out_specs, check_vma=False)
```

```python
import math

import jax
import jax.numpy as jnp
from jax import lax
from jax.experimental import pallas as pl
from jax.experimental.pallas import tpu as pltpu
from jax.sharding import PartitionSpec as P

MESH = pl.DeviceIdType.MESH
BF = jnp.bfloat16
F32 = jnp.float32
NC = 4
W = 256
STEPS = (1, 2, 3)


def dot(a, b):
    return jnp.dot(a, b, preferred_element_type=F32)


def dot_nt(a, b):
    return lax.dot_general(a, b, (((1,), (1,)), ((), ())), preferred_element_type=F32)


def kernel(
    states_h, enc_h, self_h, neigh_h, edge_h, grad_h, live, overflow,
    node_out, enc_grad,
    states, enc, w_self, w_neigh, edge, edge_f, adj, squash, feats, part, out_grad,
    core_out, core_in, zed_out, zed_in, deg_out, deg_in,
    pre, dagg, dself, hop1_in, keep, hop2_in, dzeta, rcore_in, rzed_in, rx_in, ry_in,
    sums, sums_out, last,
    load_sem, ag_s, ag_r, deg_s, deg_r, core_s, core_r, zed_s, zed_r, dg_s, dg_r, fw_s, fw_r,
    h1_s, h1_r, h2_s, h2_r, rc_s, rc_r, rz_s, rz_r, rx_s, rx_r, ry_s, ry_r,
):
    t = lax.axis_index("text")
    c = lax.axis_index("col")
    y, x, z, k = t // 4, t % 4, c // 2, c % 2
    other = 1 - k

    def at_x(d):
        return (y * 4 + (x + d) % 4, c)

    def at_y(d):
        return (((y + d) % 4) * 4 + x, c)

    def at_z(d):
        return (t, ((z + d) % 4) * 2 + k)

    def at_col(d):
        return (t, (c + d) % 8)

    sibling = (t, z * 2 + other)

    def describe(src, dst, ssem, rsem, to):
        return pltpu.make_async_remote_copy(
            src_ref=src, dst_ref=dst, send_sem=ssem, recv_sem=rsem, device_id=to,
            device_id_type=MESH,
        )

    def send(src, dst, ssem, rsem, to):
        copy = describe(src, dst, ssem, rsem, to)
        copy.start()
        return copy

    def load_states(m):
        rows = pl.ds(m * 512, 512)
        return pltpu.make_async_copy(states_h.at[rows], states.at[rows], load_sem.at[m])

    def load_enc(j):
        return pltpu.make_async_copy(enc_h.at[:, pl.ds(j * W, W)], enc.at[j], load_sem.at[8 + j])

    load_enc(0).start()
    load_states(0).start()
    rest = [
        pltpu.make_async_copy(src, dst, load_sem.at[12 + n])
        for n, (src, dst) in enumerate(
            [(edge_h, edge), (self_h, w_self), (neigh_h, w_neigh), (grad_h, out_grad)]
        )
    ]
    barrier = pltpu.get_barrier_semaphore()
    for d in STEPS:
        pl.semaphore_signal(barrier, inc=1, device_id=at_x(d), device_id_type=MESH)
        pl.semaphore_signal(barrier, inc=1, device_id=at_y(d), device_id_type=MESH)
    for d in range(1, 8):
        pl.semaphore_signal(barrier, inc=1, device_id=at_col(d), device_id_type=MESH)

    def encode(j):
        load_enc(j).wait()
        if j == 0:
            load_states(1).start()
        size = 512 if j == 0 else 1024

        def tile(m, _):
            rows = pl.ds(m * size, size)
            if j == 0:
                load_states(m).wait()

                @pl.when(m < 2)
                def _():
                    load_states(m + 2).start()

                @pl.when(m == 2)
                def _():
                    load_enc(1).start()

            s = jnp.tanh(dot(states[rows, :], enc[j]))
            squash[j, rows, :] = s
            mean = jnp.sum(s.reshape(size // 16, 16, W), axis=1) * (1.0 / 16.0)
            feats[j, y, x, pl.ds(m * (size // 16), size // 16), :] = mean.astype(BF)
            return 0

        lax.fori_loop(0, 2048 // size, tile, 0)

    LO, HI = pl.ds(0, 64), pl.ds(64, 64)

    def gather1(j):
        own_a, own_b = feats.at[j, y, x, LO], feats.at[j, y, x, HI]
        return [
            send(own_a, own_a, ag_s.at[j, d - 1], ag_r.at[j, d - 1], at_x(d)) for d in STEPS
        ] + [
            send(own_b, own_b, ag_s.at[j, 2 + d], ag_r.at[j, 2 + d], at_y(d)) for d in STEPS
        ]

    def gather2(j, first):
        for copy in first[:3]:
            copy.wait_recv()
        row = feats.at[j, y, :, LO]
        out = [
            send(row, row, ag_s.at[j, 6 + n], ag_r.at[j, 6 + n], at_y(d))
            for n, d in enumerate((1, 3))
        ]
        for copy in first[3:]:
            copy.wait_recv()
        column = feats.at[j, :, x, HI]
        return out + [
            send(column, column, ag_s.at[j, 8 + n], ag_r.at[j, 8 + n], at_x(d))
            for n, d in enumerate((1, 3))
        ]

    def gather3(j, second):
        out = []
        for n, d in enumerate((1, 3)):
            half = pl.ds(2 * n, 2)
            second[n].wait_recv()
            row = feats.at[j, (y + 4 - d) % 4, half, LO]
            out.append(send(row, row, ag_s.at[j, 10 + n], ag_r.at[j, 10 + n], at_y(d)))
            second[2 + n].wait_recv()
            column = feats.at[j, half, (x + 4 - d) % 4, HI]
            out.append(send(column, column, ag_s.at[j, 12 + n], ag_r.at[j, 12 + n], at_x(d)))
        return out

    def adjacency(r, _):
        rows = pl.ds(r * 128, 128)
        edge_f[...] = edge[rows].astype(F32).reshape(2048, 128)
        total = jnp.zeros((128, 128), F32)
        for i in range(16):
            a = edge_f[pl.ds(i, 128, stride=16), :] * live[r, i].astype(F32)
            adj[rows, i * 128 : (i + 1) * 128] = a.astype(BF)
            total = total + a
        column = jnp.broadcast_to(jnp.sum(total, axis=1, keepdims=True), (128, 128))
        deg_out[r] = column.T[0:8, :]
        return 0

    def aggregate(j, third):
        for copy in third:
            copy.wait_recv()
        p = dot(adj[...], feats[j].reshape(2048, W)).reshape(4, 2, 128, W)
        part[j] = jnp.where(k == 0, p[:, 0], p[:, 1])
        away = jnp.where(k == 0, p[:, 1], p[:, 0]).astype(BF)
        core_out[j, :, 0] = away[:, :, 0:128]
        core_out[j, :, 1] = away[:, :, 128:256]
        return send(core_out.at[j], core_in.at[j], core_s.at[j], core_r.at[j], sibling)

    def column_sum(j, copy):
        copy.wait_recv()
        for q in range(4):
            came = jnp.concatenate([core_in[j, q, 0], core_in[j, q, 1]], axis=1)
            total = part[j, q] + came.astype(F32)
            part[j, q] = total
            zed_out[j, q] = total.astype(BF)
        return [
            send(
                zed_out.at[j, (z + d) % 4], zed_in.at[j, d - 1],
                zed_s.at[j, d - 1], zed_r.at[j, d - 1], at_z(d),
            )
            for d in STEPS
        ]

    def combine(j, copies, scale):
        for copy in copies:
            copy.wait_recv()
        total = part[j, z]
        for d in range(3):
            total = total + zed_in[j, d].astype(F32)
        pooled = (total * scale).astype(BF)
        pre[...] += dot(pooled, w_neigh[pl.ds(j * W, W), :])

    encode(0)
    pl.semaphore_wait(barrier, 13)
    first, second, third = [gather1(0)], [], []
    for j in range(2, NC):
        load_enc(j).start()
    for copy in rest:
        copy.start()
    for j in range(1, NC):
        encode(j)
        first.append(gather1(j))
        second.append(gather2(j - 1, first[j - 1]))
    third.append(gather3(0, second[0]))
    rest[0].wait()
    lax.fori_loop(0, 4, adjacency, 0)
    second.append(gather2(NC - 1, first[NC - 1]))
    third.append(gather3(1, second[1]))
    lax.fori_loop(4, 8, adjacency, 0)
    deg_copies = [
        send(
            deg_out.at[(c + d) % 8], deg_in.at[d - 1], deg_s.at[d - 1], deg_r.at[d - 1], at_col(d)
        )
        for d in range(1, 8)
    ]
    def flip(m, _):
        def pair(n, _):
            a, b = pl.ds(m * 256, 256), pl.ds(n * 256, 256)
            up, down = states[a, b], states[b, a]
            states[a, b] = down.T
            states[b, a] = up.T
            return 0

        lax.fori_loop(0, m + 1, pair, 0)
        return 0

    core, zed = [aggregate(0, third[0])], []
    third.append(gather3(2, second[2]))
    third.append(gather3(3, second[3]))
    core.append(aggregate(1, third[1]))
    zed.append(column_sum(0, core[0]))
    core.append(aggregate(2, third[2]))
    zed.append(column_sum(1, core[1]))
    for copy in rest[1:]:
        copy.wait()
    own = jnp.concatenate([feats[j, y, x] for j in range(NC)], axis=1)
    pre[...] = dot(own, w_self[...])
    for copy in deg_copies:
        copy.wait_recv()
    degree = deg_out[c]
    for d in range(7):
        degree = degree + deg_in[d]
    inv_row = lax.rsqrt(1.0 + degree)[0:1, :]
    inv_column = jnp.broadcast_to(inv_row, (128, 128)).T[:, 0:1]
    combine(0, zed[0], inv_column)
    core.append(aggregate(3, third[3]))
    zed.append(column_sum(2, core[2]))
    combine(1, zed[1], inv_column)
    lax.fori_loop(0, 3, flip, 0)
    zed.append(column_sum(3, core[3]))
    combine(2, zed[2], inv_column)
    lax.fori_loop(3, 6, flip, 0)
    combine(3, zed[3], inv_column)

    v = pre[...]
    sg = 1.0 / (1.0 + jnp.exp(-v))
    node_out[...] = (v * sg).astype(BF)
    dpre = (out_grad[...].astype(F32) * sg * (1.0 + v * (1.0 - sg))).astype(BF)

    around = []

    def spread(j):
        dagg[j, c] = (dot_nt(w_neigh[pl.ds(j * W, W), :], dpre) * inv_row).astype(BF)
        own = dagg.at[j, c]
        around.append(
            [send(own, own, dg_s.at[j, d - 1], dg_r.at[j, d - 1], at_z(d)) for d in STEPS]
            + [send(own, own, dg_s.at[j, 3], dg_r.at[j, 3], sibling)]
        )

    spread(0)
    for j in range(NC):
        dself[j] = dot_nt(w_self[pl.ds(j * W, W), :], dpre)
    lax.fori_loop(6, 8, flip, 0)

    for copies in first + second + third + zed:
        for copy in copies:
            copy.wait_send()
    for copy in core + deg_copies:
        copy.wait_send()

    def forward(j):
        out = []
        for d in STEPS:
            around[j][d - 1].wait_recv()
            block = dagg.at[j, ((z - d + 4) % 4) * 2 + k]
            out.append(send(block, block, fw_s.at[j, d - 1], fw_r.at[j, d - 1], sibling))
        return out

    def piece(j, half, major, minor, blocks):
        return pl.ds(((j * 2 + half) * 16 + major * 4 + minor) * 8, blocks * 8)

    def transpose_product(j, passed):
        around[j][3].wait_recv()
        for copy in passed:
            copy.wait_recv()
        chunk = jnp.concatenate([dagg[j, q] for q in range(8)], axis=1)
        p = dot(chunk, adj[...]).astype(BF)
        for i in range(16):
            yy, xx, lanes = i // 4, i % 4, slice(i * 128, (i + 1) * 128)
            edge[piece(j, 0, yy, xx, 1)] = p[0:128, lanes].reshape(8, 16, 128)
            edge[piece(j, 1, xx, yy, 1)] = p[128:256, lanes].reshape(8, 16, 128)

    WAYS = ((1, 0, 2), (3, 2, 0))

    def scatter1(j):
        relayed, direct = [], []
        for n, (d, via, straight) in enumerate(WAYS):
            into = pl.ds(2 * n * 8, 16)
            for half, at, place in ((0, at_y, y), (1, at_x, x)):
                relayed.append(
                    send(
                        edge.at[piece(j, half, (place + 2) % 4, via, 2)],
                        hop1_in.at[j, half, 2, into],
                        h1_s.at[j, 2 * n + half], h1_r.at[j, 2 * n + half], at(d),
                    )
                )
        for n, (d, via, straight) in enumerate(WAYS):
            into = pl.ds(straight * 8, 16)
            for half, at, place in ((0, at_y, y), (1, at_x, x)):
                direct.append(
                    send(
                        edge.at[piece(j, half, (place + d) % 4, straight, 2)],
                        hop1_in.at[j, half, n, into],
                        h1_s.at[j, 4 + 2 * n + half], h1_r.at[j, 4 + 2 * n + half], at(d),
                    )
                )
        return relayed, direct

    def relay(j, relayed):
        out = []
        for n, (d, via, _) in enumerate(WAYS):
            for half, at, place in ((0, at_y, y), (1, at_x, x)):
                relayed[2 * n + half].wait_recv()
                mine = piece(j, half, (place + d) % 4, via, 2)
                came = hop1_in[j, half, 2, pl.ds(2 * n * 8, 16)].astype(F32)
                edge[mine] = (edge[mine].astype(F32) + came).astype(BF)
                out.append(
                    send(
                        edge.at[mine], hop1_in.at[j, half, n, pl.ds(via * 8, 16)],
                        h1_s.at[j, 8 + 2 * n + half], h1_r.at[j, 8 + 2 * n + half], at(d),
                    )
                )
        return out

    def scatter2(j, copies):
        for copy in copies:
            copy.wait_recv()
        for q in range(4):
            for half, place in ((0, y), (1, x)):
                total = edge[piece(j, half, place, q, 1)].astype(F32)
                for n in range(2):
                    total = total + hop1_in[j, half, n, pl.ds(q * 8, 8)].astype(F32)
                total = total.reshape(128, 128)
                part[0, q, :, half * 128 : half * 128 + 128] = total
                core_out[j, q, half] = total.astype(BF)
        keep[j, 0] = part[0, x, :, 0:128]
        keep[j, 1] = part[0, y, :, 128:256]
        out = []
        for d in STEPS:
            out.append(
                send(
                    core_out.at[j, (x + d) % 4, 0], hop2_in.at[j, 0, d - 1],
                    h2_s.at[j, d - 1], h2_r.at[j, d - 1], at_x(d),
                )
            )
            out.append(
                send(
                    core_out.at[j, (y + d) % 4, 1], hop2_in.at[j, 1, d - 1],
                    h2_s.at[j, 2 + d], h2_r.at[j, 2 + d], at_y(d),
                )
            )
        return out

    def encoder_term(j, copies):
        for copy in copies:
            copy.wait_recv()
        halves = []
        for h in range(2):
            total = keep[j, h]
            for d in range(3):
                total = total + hop2_in[j, h, d].astype(F32)
            halves.append(total)
        dx0 = jnp.concatenate(halves, axis=0) + dself[j]
        part[1, 0] = dx0.T * (1.0 / 16.0)

        def tile(m, _):
            rows = pl.ds(m * 256, 256)
            s = squash[j, rows, :].reshape(16, 16, W)
            g = part[1, 0, pl.ds(m * 16, 16), :].reshape(16, 1, W)
            dzeta[rows, :] = (g * (1.0 - s * s)).astype(BF).reshape(256, W)
            return 0

        lax.fori_loop(0, 8, tile, 0)

        def term(m, _):
            rows = pl.ds(m * 1024, 1024)
            squash[j, rows, :] = dot(states[rows, :], dzeta[...])
            for g in range(32):
                away = squash[j, pl.ds(m * 1024 + g * 32 + other * 16, 16), :].astype(BF)
                enc[j, pl.ds(m * 512 + g * 16, 16), :] = away
            raw_half(j, m).start()
            return 0

        lax.fori_loop(0, 2, term, 0)

    def raw_half(j, m):
        rows = pl.ds(m * 512, 512)
        return describe(
            enc.at[j, rows], rcore_in.at[j, rows], rc_s.at[j, m], rc_r.at[j, m], sibling
        )

    def term_zed(j, half):
        raw_half(j, half).wait_recv()
        base = 1024 + half * 512

        def tile(m, _):
            for q in range(4):
                g = m * 4 + q
                mine = pl.ds(g * 32 + k * 16, 16)
                total = squash[j, mine, :] + rcore_in[j, pl.ds(g * 16, 16), :].astype(F32)
                squash[j, mine, :] = total
                if half == 0:
                    slot = q * 128 + m * 16
                else:
                    slot = (m % 4) * 128 + ((m // 4 - 2) * 4 + q) * 16
                enc[j, pl.ds(base + slot, 16), :] = total.astype(BF)
            return 0

        lax.fori_loop(half * 8, half * 8 + 8, tile, 0)
        place, at = ((z, at_z), (x, at_x))[half]
        into = pl.ds(half * 128, 128)
        return [
            send(
                enc.at[j, pl.ds(base + ((place + d) % 4) * 128, 128)],
                rzed_in.at[j, d - 1, into],
                rz_s.at[j, half * 3 + d - 1], rz_r.at[j, half * 3 + d - 1], at(d),
            )
            for d in STEPS
        ]

    def term_x(j, half, copies):
        for copy in copies:
            copy.wait_recv()

        def tile(m, _):
            if half == 0:
                row = (m * 4 + z) * 32
                slot = (m % 4) * 32 + (m // 4) * 16
            else:
                row = (((2 + m // 4) * 4 + x) * 4 + m % 4) * 32
                slot = 128 + (m % 4) * 32 + (m // 4) * 16
            total = squash[j, pl.ds(row + k * 16, 16), :]
            for d in range(3):
                came = rzed_in[j, d, pl.ds(half * 128 + m * 16, 16), :]
                total = total + came.astype(F32)
            sums[j, pl.ds(slot, 16), :] = total
            sums_out[j, pl.ds(slot, 16), :] = total.astype(BF)
            return 0

        lax.fori_loop(0, 8, tile, 0)
        place, at = ((x, at_x), (z, at_z))[half]
        return [
            send(
                sums_out.at[j, pl.ds(half * 128 + ((place + d) % 4) * 32, 32)],
                rx_in.at[j, half, d - 1],
                rx_s.at[j, half * 3 + d - 1], rx_r.at[j, half * 3 + d - 1], at(d),
            )
            for d in STEPS
        ]

    def term_y(j, copies):
        for copy in copies:
            copy.wait_recv()
        for half, place in ((0, x), (1, z)):
            total = sums[j, pl.ds(half * 128 + place * 32, 32), :]
            for d in range(3):
                total = total + rx_in[j, half, d].astype(F32)
            last[j, half * 32 : half * 32 + 32, :] = total
        return [
            send(
                last.at[j, pl.ds(((y + d) % 4) * 16, 16)], ry_in.at[j, d - 1],
                ry_s.at[j, d - 1], ry_r.at[j, d - 1], at_y(d),
            )
            for d in STEPS
        ]

    factor = 1024.0 / (1024.0 + overflow[0].astype(F32)) * (16.0 / math.sqrt(16384 * 16))

    def finish(j, copies):
        for copy in copies:
            copy.wait_recv()
        total = last[j, pl.ds(y * 16, 16), :]
        for d in range(3):
            total = total + ry_in[j, d]
        enc_grad[:, j * W : (j + 1) * W] = total * factor

    passed, relayed, direct, hop1 = [], [], [], []
    hop2, rzed, rx, ry = [], [], [], []

    def product(j):
        passed.append(forward(j))
        if j + 1 < NC:
            spread(j + 1)
        transpose_product(j, passed[j])

    def first_hop(j):
        for kept, copies in zip((relayed, direct), scatter1(j)):
            kept.append(copies)

    def pass_on(j):
        hop1.append(relay(j, relayed[j]))

    def second_hop(j):
        hop2.append(scatter2(j, direct[j] + hop1[j]))

    def raw(j):
        encoder_term(j, hop2[j])

    def raw_z(j):
        rzed.append(term_zed(j, 0) + term_zed(j, 1))

    def raw_x(j):
        rx.append(term_x(j, 0, rzed[j][:3]) + term_x(j, 1, rzed[j][3:]))

    def raw_y(j):
        ry.append(term_y(j, rx[j]))

    for step, j in (
        (product, 0), (first_hop, 0), (product, 1), (pass_on, 0), (first_hop, 1), (product, 2),
        (pass_on, 1), (second_hop, 0), (first_hop, 2), (product, 3), (first_hop, 3),
        (second_hop, 1), (pass_on, 2), (raw, 0), (pass_on, 3), (second_hop, 2), (raw_z, 0),
        (raw, 1), (second_hop, 3), (raw_z, 1), (raw_x, 0), (raw, 2), (raw_z, 2), (raw_x, 1),
        (raw_y, 0), (raw, 3), (raw_x, 2), (raw_y, 1), (raw_z, 3), (raw_y, 2), (raw_x, 3),
        (raw_y, 3),
    ):
        step(j)
    for j in range(NC):
        finish(j, ry[j])

    for copies in around + passed + relayed + direct + hop1 + hop2 + rzed + rx + ry:
        for copy in copies:
            copy.wait_send()
    for j in range(NC):
        for half in range(2):
            raw_half(j, half).wait_send()


def hand_over(a, b, a_out, b_out):
    a_out[...] = a[...]
    b_out[...] = b[...]


def local(
    states, enc_weight, self_weight, neighbour_weight, edge_weight, tile_live, out_grad, overflow
):
    states = states.reshape(2048, 2048)
    edge_weight = edge_weight.reshape(1024, 16, 128)
    tile_live = tile_live.reshape(8, 16)
    hbm = pl.BlockSpec(memory_space=pl.ANY)
    smem = pl.BlockSpec(memory_space=pltpu.SMEM)
    vmem = pl.BlockSpec(memory_space=pltpu.VMEM)
    V, S = pltpu.VMEM, pltpu.SemaphoreType.DMA
    buffers = [
        V((2048, 2048), BF),
        V((NC, 2048, W), BF),
        V((1024, 1024), BF),
        V((1024, 1024), BF),
        V((1024, 16, 128), BF),
        V((2048, 128), F32),
        V((1024, 2048), BF),
        V((NC, 2048, W), F32),
        V((NC, 4, 4, 128, W), BF),
        V((NC, 4, 128, W), F32),
        V((128, 1024), BF),
        V((NC, 4, 2, 128, 128), BF),
        V((NC, 4, 2, 128, 128), BF),
        V((NC, 4, 128, W), BF),
        V((NC, 3, 128, W), BF),
        V((8, 8, 128), F32),
        V((7, 8, 128), F32),
        V((128, 1024), F32),
        V((NC, 8, W, 128), BF),
        V((NC, W, 128), F32),
        V((NC, 2, 3, 32, 16, 128), BF),
        V((NC, 2, 128, 128), F32),
        V((NC, 2, 3, 128, 128), BF),
        V((2048, W), BF),
        V((NC, 1024, W), BF),
        V((NC, 3, 256, W), BF),
        V((NC, 2, 3, 32, W), BF),
        V((NC, 3, 16, W), F32),
        V((NC, 256, W), F32),
        V((NC, 256, W), BF),
        V((NC, 64, W), F32),
    ]
    shapes = [
        (NC, 14), (7,), (NC,), (NC, 3), (NC, 4), (NC, 3), (NC, 12), (NC, 6), (NC, 2), (NC, 6),
        (NC, 6), (NC, 3),
    ]
    semaphores = [S((16,))] + [S(shape) for shape in shapes for _ in range(2)]
    results = pl.pallas_call(
        kernel,
        out_shape=(
            jax.ShapeDtypeStruct((128, 1024), BF),
            jax.ShapeDtypeStruct((16, 1024), F32),
        ),
        in_specs=[hbm] * 6 + [smem] * 2,
        out_specs=(vmem, vmem),
        scratch_shapes=buffers + semaphores,
        compiler_params=pltpu.CompilerParams(
            collective_id=0, has_side_effects=True, vmem_limit_bytes=63 * 1024 * 1024
        ),
        name="step",
    )(states, enc_weight, self_weight, neighbour_weight, edge_weight, out_grad, tile_live, overflow)
    return pl.pallas_call(
        hand_over,
        out_shape=tuple(jax.ShapeDtypeStruct(r.shape, r.dtype) for r in results),
        in_specs=[vmem] * 2,
        out_specs=(vmem,) * 2,
        name="hand_over",
    )(*results)


def solution(mesh):
    in_specs = (
        P(("text", "col"), None, None),
        P(),
        P(),
        P(),
        P("text", "col", None, None),
        P("text", "col", None),
        P(("text", "col"), None),
        P(),
    )
    out_specs = (P(("text", "col"), None), P(("text", "col"), None))
    return jax.shard_map(local, mesh=mesh, in_specs=in_specs, out_specs=out_specs, check_vma=False)
```

```python
import math

import jax
import jax.numpy as jnp
from jax import lax
from jax.experimental import pallas as pl
from jax.experimental.pallas import tpu as pltpu
from jax.sharding import PartitionSpec as P

MESH = pl.DeviceIdType.MESH
BF = jnp.bfloat16
F32 = jnp.float32
NC = 4
W = 256
STEPS = (1, 2, 3)


def dot(a, b):
    return jnp.dot(a, b, preferred_element_type=F32)


def dot_nt(a, b):
    return lax.dot_general(a, b, (((1,), (1,)), ((), ())), preferred_element_type=F32)


def kernel(
    states_h, enc_h, self_h, neigh_h, edge_h, grad_h, live, overflow,
    node_out, enc_grad,
    states, enc, w_self, w_neigh, edge, edge_f, adj, squash, feats, part, out_grad,
    core_out, core_in, zed_out, zed_in, deg_out, deg_in,
    pre, dagg, dself, hop1_in, keep, hop2_in, dzeta, rcore_in, rzed_in, rx_in, ry_in,
    sums, sums_out, last,
    load_sem, ag_s, ag_r, deg_s, deg_r, core_s, core_r, zed_s, zed_r, dg_s, dg_r, fw_s, fw_r,
    h1_s, h1_r, h2_s, h2_r, rc_s, rc_r, rz_s, rz_r, rx_s, rx_r, ry_s, ry_r,
):
    t = lax.axis_index("text")
    c = lax.axis_index("col")
    y, x, z, k = t // 4, t % 4, c // 2, c % 2
    other = 1 - k

    def at_x(d):
        return (y * 4 + (x + d) % 4, c)

    def at_y(d):
        return (((y + d) % 4) * 4 + x, c)

    def at_z(d):
        return (t, ((z + d) % 4) * 2 + k)

    def at_col(d):
        return (t, (c + d) % 8)

    sibling = (t, z * 2 + other)

    def describe(src, dst, ssem, rsem, to):
        return pltpu.make_async_remote_copy(
            src_ref=src, dst_ref=dst, send_sem=ssem, recv_sem=rsem, device_id=to,
            device_id_type=MESH,
        )

    def send(src, dst, ssem, rsem, to):
        copy = describe(src, dst, ssem, rsem, to)
        copy.start()
        return copy

    def load_states(m):
        rows = pl.ds(m * 512, 512)
        return pltpu.make_async_copy(states_h.at[rows], states.at[rows], load_sem.at[m])

    def load_enc(j):
        return pltpu.make_async_copy(enc_h.at[:, pl.ds(j * W, W)], enc.at[j], load_sem.at[8 + j])

    load_enc(0).start()
    load_states(0).start()
    rest = [
        pltpu.make_async_copy(src, dst, load_sem.at[12 + n])
        for n, (src, dst) in enumerate(
            [(edge_h, edge), (self_h, w_self), (neigh_h, w_neigh), (grad_h, out_grad)]
        )
    ]
    barrier = pltpu.get_barrier_semaphore()
    for d in STEPS:
        pl.semaphore_signal(barrier, inc=1, device_id=at_x(d), device_id_type=MESH)
        pl.semaphore_signal(barrier, inc=1, device_id=at_y(d), device_id_type=MESH)
    for d in range(1, 8):
        pl.semaphore_signal(barrier, inc=1, device_id=at_col(d), device_id_type=MESH)

    def encode(j):
        load_enc(j).wait()
        if j == 0:
            load_states(1).start()
        size = 512 if j == 0 else 1024

        def tile(m, _):
            rows = pl.ds(m * size, size)
            if j == 0:
                load_states(m).wait()

                @pl.when(m < 2)
                def _():
                    load_states(m + 2).start()

                @pl.when(m == 2)
                def _():
                    load_enc(1).start()

            s = jnp.tanh(dot(states[rows, :], enc[j]))
            squash[j, rows, :] = s
            mean = jnp.sum(s.reshape(size // 16, 16, W), axis=1) * (1.0 / 16.0)
            feats[j, y, x, pl.ds(m * (size // 16), size // 16), :] = mean.astype(BF)
            return 0

        lax.fori_loop(0, 2048 // size, tile, 0)

    LO, HI = pl.ds(0, 64), pl.ds(64, 64)

    def gather1(j):
        own_a, own_b = feats.at[j, y, x, LO], feats.at[j, y, x, HI]
        return [
            send(own_a, own_a, ag_s.at[j, d - 1], ag_r.at[j, d - 1], at_x(d)) for d in STEPS
        ] + [
            send(own_b, own_b, ag_s.at[j, 2 + d], ag_r.at[j, 2 + d], at_y(d)) for d in STEPS
        ]

    def gather2(j, first):
        for copy in first[:3]:
            copy.wait_recv()
        row = feats.at[j, y, :, LO]
        out = [
            send(row, row, ag_s.at[j, 6 + n], ag_r.at[j, 6 + n], at_y(d))
            for n, d in enumerate((1, 3))
        ]
        for copy in first[3:]:
            copy.wait_recv()
        column = feats.at[j, :, x, HI]
        return out + [
            send(column, column, ag_s.at[j, 8 + n], ag_r.at[j, 8 + n], at_x(d))
            for n, d in enumerate((1, 3))
        ]

    def gather3(j, second):
        out = []
        for n, d in enumerate((1, 3)):
            half = pl.ds(2 * n, 2)
            second[n].wait_recv()
            row = feats.at[j, (y + 4 - d) % 4, half, LO]
            out.append(send(row, row, ag_s.at[j, 10 + n], ag_r.at[j, 10 + n], at_y(d)))
            second[2 + n].wait_recv()
            column = feats.at[j, half, (x + 4 - d) % 4, HI]
            out.append(send(column, column, ag_s.at[j, 12 + n], ag_r.at[j, 12 + n], at_x(d)))
        return out

    def adjacency(r, _):
        rows = pl.ds(r * 128, 128)
        edge_f[...] = edge[rows].astype(F32).reshape(2048, 128)
        total = jnp.zeros((128, 128), F32)
        for i in range(16):
            a = edge_f[pl.ds(i, 128, stride=16), :] * live[r, i].astype(F32)
            adj[rows, i * 128 : (i + 1) * 128] = a.astype(BF)
            total = total + a
        column = jnp.broadcast_to(jnp.sum(total, axis=1, keepdims=True), (128, 128))
        deg_out[r] = column.T[0:8, :]
        return 0

    def aggregate(j, third):
        for copy in third:
            copy.wait_recv()
        p = dot(adj[...], feats[j].reshape(2048, W)).reshape(4, 2, 128, W)
        part[j] = jnp.where(k == 0, p[:, 0], p[:, 1])
        away = jnp.where(k == 0, p[:, 1], p[:, 0]).astype(BF)
        core_out[j, :, 0] = away[:, :, 0:128]
        core_out[j, :, 1] = away[:, :, 128:256]
        return send(core_out.at[j], core_in.at[j], core_s.at[j], core_r.at[j], sibling)

    def column_sum(j, copy):
        copy.wait_recv()
        for q in range(4):
            came = jnp.concatenate([core_in[j, q, 0], core_in[j, q, 1]], axis=1)
            total = part[j, q] + came.astype(F32)
            part[j, q] = total
            zed_out[j, q] = total.astype(BF)
        return [
            send(
                zed_out.at[j, (z + d) % 4], zed_in.at[j, d - 1],
                zed_s.at[j, d - 1], zed_r.at[j, d - 1], at_z(d),
            )
            for d in STEPS
        ]

    def combine(j, copies, scale):
        for copy in copies:
            copy.wait_recv()
        total = part[j, z]
        for d in range(3):
            total = total + zed_in[j, d].astype(F32)
        pooled = (total * scale).astype(BF)
        pre[...] += dot(pooled, w_neigh[pl.ds(j * W, W), :])

    encode(0)
    pl.semaphore_wait(barrier, 13)
    first, second, third = [gather1(0)], [], []
    for j in range(2, NC):
        load_enc(j).start()
    for copy in rest:
        copy.start()
    for j in range(1, NC):
        encode(j)
        first.append(gather1(j))
        second.append(gather2(j - 1, first[j - 1]))
    third.append(gather3(0, second[0]))
    rest[0].wait()
    lax.fori_loop(0, 4, adjacency, 0)
    second.append(gather2(NC - 1, first[NC - 1]))
    third.append(gather3(1, second[1]))
    lax.fori_loop(4, 8, adjacency, 0)
    deg_copies = [
        send(
            deg_out.at[(c + d) % 8], deg_in.at[d - 1], deg_s.at[d - 1], deg_r.at[d - 1], at_col(d)
        )
        for d in range(1, 8)
    ]
    def flip(m, _):
        def pair(n, _):
            a, b = pl.ds(m * 256, 256), pl.ds(n * 256, 256)
            up, down = states[a, b], states[b, a]
            states[a, b] = down.T
            states[b, a] = up.T
            return 0

        lax.fori_loop(0, m + 1, pair, 0)
        return 0

    core, zed = [aggregate(0, third[0])], []
    third.append(gather3(2, second[2]))
    third.append(gather3(3, second[3]))
    core.append(aggregate(1, third[1]))
    zed.append(column_sum(0, core[0]))
    core.append(aggregate(2, third[2]))
    zed.append(column_sum(1, core[1]))
    for copy in rest[1:]:
        copy.wait()
    own = jnp.concatenate([feats[j, y, x] for j in range(NC)], axis=1)
    pre[...] = dot(own, w_self[...])
    for copy in deg_copies:
        copy.wait_recv()
    degree = deg_out[c]
    for d in range(7):
        degree = degree + deg_in[d]
    inv_row = lax.rsqrt(1.0 + degree)[0:1, :]
    inv_column = jnp.broadcast_to(inv_row, (128, 128)).T[:, 0:1]
    combine(0, zed[0], inv_column)
    core.append(aggregate(3, third[3]))
    zed.append(column_sum(2, core[2]))
    combine(1, zed[1], inv_column)
    lax.fori_loop(0, 3, flip, 0)
    zed.append(column_sum(3, core[3]))
    combine(2, zed[2], inv_column)
    lax.fori_loop(3, 6, flip, 0)
    combine(3, zed[3], inv_column)

    v = pre[...]
    sg = 1.0 / (1.0 + jnp.exp(-v))
    node_out[...] = (v * sg).astype(BF)
    dpre = (out_grad[...].astype(F32) * sg * (1.0 + v * (1.0 - sg))).astype(BF)

    around = []

    def spread(j):
        dagg[j, c] = (dot_nt(w_neigh[pl.ds(j * W, W), :], dpre) * inv_row).astype(BF)
        own = dagg.at[j, c]
        around.append(
            [send(own, own, dg_s.at[j, d - 1], dg_r.at[j, d - 1], at_z(d)) for d in STEPS]
            + [send(own, own, dg_s.at[j, 3], dg_r.at[j, 3], sibling)]
        )

    spread(0)
    for j in range(NC):
        dself[j] = dot_nt(w_self[pl.ds(j * W, W), :], dpre)
    lax.fori_loop(6, 8, flip, 0)
    spread(1)

    for copies in first + second + third + zed:
        for copy in copies:
            copy.wait_send()
    for copy in core + deg_copies:
        copy.wait_send()

    def forward(j):
        out = []
        for d in STEPS:
            around[j][d - 1].wait_recv()
            block = dagg.at[j, ((z - d + 4) % 4) * 2 + k]
            out.append(send(block, block, fw_s.at[j, d - 1], fw_r.at[j, d - 1], sibling))
        return out

    def piece(j, half, major, minor, blocks):
        return pl.ds(((j * 2 + half) * 16 + major * 4 + minor) * 8, blocks * 8)

    def transpose_product(j, passed):
        around[j][3].wait_recv()
        for copy in passed:
            copy.wait_recv()
        chunk = jnp.concatenate([dagg[j, q] for q in range(8)], axis=1)
        p = dot(chunk, adj[...]).astype(BF)
        for i in range(16):
            yy, xx, lanes = i // 4, i % 4, slice(i * 128, (i + 1) * 128)
            edge[piece(j, 0, yy, xx, 1)] = p[0:128, lanes].reshape(8, 16, 128)
            edge[piece(j, 1, xx, yy, 1)] = p[128:256, lanes].reshape(8, 16, 128)

    WAYS = ((1, 0, 2), (3, 2, 0))

    def scatter1(j):
        relayed, direct = [], []
        for n, (d, via, straight) in enumerate(WAYS):
            into = pl.ds(2 * n * 8, 16)
            for half, at, place in ((0, at_y, y), (1, at_x, x)):
                relayed.append(
                    send(
                        edge.at[piece(j, half, (place + 2) % 4, via, 2)],
                        hop1_in.at[j, half, 2, into],
                        h1_s.at[j, 2 * n + half], h1_r.at[j, 2 * n + half], at(d),
                    )
                )
        for n, (d, via, straight) in enumerate(WAYS):
            into = pl.ds(straight * 8, 16)
            for half, at, place in ((0, at_y, y), (1, at_x, x)):
                direct.append(
                    send(
                        edge.at[piece(j, half, (place + d) % 4, straight, 2)],
                        hop1_in.at[j, half, n, into],
                        h1_s.at[j, 4 + 2 * n + half], h1_r.at[j, 4 + 2 * n + half], at(d),
                    )
                )
        return relayed, direct

    def relay(j, relayed):
        out = []
        for n, (d, via, _) in enumerate(WAYS):
            for half, at, place in ((0, at_y, y), (1, at_x, x)):
                relayed[2 * n + half].wait_recv()
                mine = piece(j, half, (place + d) % 4, via, 2)
                came = hop1_in[j, half, 2, pl.ds(2 * n * 8, 16)].astype(F32)
                edge[mine] = (edge[mine].astype(F32) + came).astype(BF)
                out.append(
                    send(
                        edge.at[mine], hop1_in.at[j, half, n, pl.ds(via * 8, 16)],
                        h1_s.at[j, 8 + 2 * n + half], h1_r.at[j, 8 + 2 * n + half], at(d),
                    )
                )
        return out

    def scatter2(j, copies):
        for copy in copies:
            copy.wait_recv()
        for q in range(4):
            for half, place in ((0, y), (1, x)):
                total = edge[piece(j, half, place, q, 1)].astype(F32)
                for n in range(2):
                    total = total + hop1_in[j, half, n, pl.ds(q * 8, 8)].astype(F32)
                total = total.reshape(128, 128)
                part[0, q, :, half * 128 : half * 128 + 128] = total
                core_out[j, q, half] = total.astype(BF)
        keep[j, 0] = part[0, x, :, 0:128]
        keep[j, 1] = part[0, y, :, 128:256]
        out = []
        for d in STEPS:
            out.append(
                send(
                    core_out.at[j, (x + d) % 4, 0], hop2_in.at[j, 0, d - 1],
                    h2_s.at[j, d - 1], h2_r.at[j, d - 1], at_x(d),
                )
            )
            out.append(
                send(
                    core_out.at[j, (y + d) % 4, 1], hop2_in.at[j, 1, d - 1],
                    h2_s.at[j, 2 + d], h2_r.at[j, 2 + d], at_y(d),
                )
            )
        return out

    def encoder_term(j, copies):
        for copy in copies:
            copy.wait_recv()
        halves = []
        for h in range(2):
            total = keep[j, h]
            for d in range(3):
                total = total + hop2_in[j, h, d].astype(F32)
            halves.append(total)
        dx0 = jnp.concatenate(halves, axis=0) + dself[j]
        part[1, 0] = dx0.T * (1.0 / 16.0)

        def tile(m, _):
            rows = pl.ds(m * 256, 256)
            s = squash[j, rows, :].reshape(16, 16, W)
            g = part[1, 0, pl.ds(m * 16, 16), :].reshape(16, 1, W)
            dzeta[rows, :] = (g * (1.0 - s * s)).astype(BF).reshape(256, W)
            return 0

        lax.fori_loop(0, 8, tile, 0)

        def term(m, _):
            rows = pl.ds(m * 1024, 1024)
            squash[j, rows, :] = dot(states[rows, :], dzeta[...])
            for g in range(32):
                away = squash[j, pl.ds(m * 1024 + g * 32 + other * 16, 16), :].astype(BF)
                enc[j, pl.ds(m * 512 + g * 16, 16), :] = away
            raw_half(j, m).start()
            return 0

        lax.fori_loop(0, 2, term, 0)

    def raw_half(j, m):
        rows = pl.ds(m * 512, 512)
        return describe(
            enc.at[j, rows], rcore_in.at[j, rows], rc_s.at[j, m], rc_r.at[j, m], sibling
        )

    def term_zed(j, half):
        raw_half(j, half).wait_recv()
        base = 1024 + half * 512

        def tile(m, _):
            for q in range(4):
                g = m * 4 + q
                mine = pl.ds(g * 32 + k * 16, 16)
                total = squash[j, mine, :] + rcore_in[j, pl.ds(g * 16, 16), :].astype(F32)
                squash[j, mine, :] = total
                if half == 0:
                    slot = q * 128 + m * 16
                else:
                    slot = (m % 4) * 128 + ((m // 4 - 2) * 4 + q) * 16
                enc[j, pl.ds(base + slot, 16), :] = total.astype(BF)
            return 0

        lax.fori_loop(half * 8, half * 8 + 8, tile, 0)
        place, at = ((z, at_z), (x, at_x))[half]
        into = pl.ds(half * 128, 128)
        return [
            send(
                enc.at[j, pl.ds(base + ((place + d) % 4) * 128, 128)],
                rzed_in.at[j, d - 1, into],
                rz_s.at[j, half * 3 + d - 1], rz_r.at[j, half * 3 + d - 1], at(d),
            )
            for d in STEPS
        ]

    def term_x(j, half, copies):
        for copy in copies:
            copy.wait_recv()

        def tile(m, _):
            if half == 0:
                row = (m * 4 + z) * 32
                slot = (m % 4) * 32 + (m // 4) * 16
            else:
                row = (((2 + m // 4) * 4 + x) * 4 + m % 4) * 32
                slot = 128 + (m % 4) * 32 + (m // 4) * 16
            total = squash[j, pl.ds(row + k * 16, 16), :]
            for d in range(3):
                came = rzed_in[j, d, pl.ds(half * 128 + m * 16, 16), :]
                total = total + came.astype(F32)
            sums[j, pl.ds(slot, 16), :] = total
            sums_out[j, pl.ds(slot, 16), :] = total.astype(BF)
            return 0

        lax.fori_loop(0, 8, tile, 0)
        place, at = ((x, at_x), (z, at_z))[half]
        return [
            send(
                sums_out.at[j, pl.ds(half * 128 + ((place + d) % 4) * 32, 32)],
                rx_in.at[j, half, d - 1],
                rx_s.at[j, half * 3 + d - 1], rx_r.at[j, half * 3 + d - 1], at(d),
            )
            for d in STEPS
        ]

    def term_y(j, copies):
        for copy in copies:
            copy.wait_recv()
        for half, place in ((0, x), (1, z)):
            total = sums[j, pl.ds(half * 128 + place * 32, 32), :]
            for d in range(3):
                total = total + rx_in[j, half, d].astype(F32)
            last[j, half * 32 : half * 32 + 32, :] = total
        return [
            send(
                last.at[j, pl.ds(((y + d) % 4) * 16, 16)], ry_in.at[j, d - 1],
                ry_s.at[j, d - 1], ry_r.at[j, d - 1], at_y(d),
            )
            for d in STEPS
        ]

    factor = 1024.0 / (1024.0 + overflow[0].astype(F32)) * (16.0 / math.sqrt(16384 * 16))

    def finish(j, copies):
        for copy in copies:
            copy.wait_recv()
        total = last[j, pl.ds(y * 16, 16), :]
        for d in range(3):
            total = total + ry_in[j, d]
        enc_grad[:, j * W : (j + 1) * W] = total * factor

    passed, relayed, direct, hop1 = [], [], [], []
    hop2, rzed, rx, ry = [], [], [], []

    def product(j):
        passed.append(forward(j))
        if j + 2 < NC:
            spread(j + 2)
        transpose_product(j, passed[j])

    def first_hop(j):
        for kept, copies in zip((relayed, direct), scatter1(j)):
            kept.append(copies)

    def pass_on(j):
        hop1.append(relay(j, relayed[j]))

    def second_hop(j):
        hop2.append(scatter2(j, direct[j] + hop1[j]))

    def raw(j):
        encoder_term(j, hop2[j])

    def raw_z(j):
        rzed.append(term_zed(j, 0) + term_zed(j, 1))

    def raw_x(j):
        rx.append(term_x(j, 0, rzed[j][:3]) + term_x(j, 1, rzed[j][3:]))

    def raw_y(j):
        ry.append(term_y(j, rx[j]))

    for step, j in (
        (product, 0), (first_hop, 0), (product, 1), (first_hop, 1), (pass_on, 0), (product, 2),
        (first_hop, 2), (pass_on, 1), (product, 3), (first_hop, 3), (second_hop, 0), (pass_on, 2),
        (second_hop, 1), (pass_on, 3), (raw, 0), (second_hop, 2), (second_hop, 3), (raw_z, 0),
        (raw, 1), (raw_z, 1), (raw_x, 0), (raw, 2), (raw_z, 2), (raw_x, 1), (raw_y, 0), (raw, 3),
        (raw_x, 2), (raw_y, 1), (raw_z, 3), (raw_y, 2), (raw_x, 3), (raw_y, 3),
    ):
        step(j)
    for j in range(NC):
        finish(j, ry[j])

    for copies in around + passed + relayed + direct + hop1 + hop2 + rzed + rx + ry:
        for copy in copies:
            copy.wait_send()
    for j in range(NC):
        for half in range(2):
            raw_half(j, half).wait_send()


def hand_over(a, b, a_out, b_out):
    a_out[...] = a[...]
    b_out[...] = b[...]


def local(
    states, enc_weight, self_weight, neighbour_weight, edge_weight, tile_live, out_grad, overflow
):
    states = states.reshape(2048, 2048)
    edge_weight = edge_weight.reshape(1024, 16, 128)
    tile_live = tile_live.reshape(8, 16)
    hbm = pl.BlockSpec(memory_space=pl.ANY)
    smem = pl.BlockSpec(memory_space=pltpu.SMEM)
    vmem = pl.BlockSpec(memory_space=pltpu.VMEM)
    V, S = pltpu.VMEM, pltpu.SemaphoreType.DMA
    buffers = [
        V((2048, 2048), BF),
        V((NC, 2048, W), BF),
        V((1024, 1024), BF),
        V((1024, 1024), BF),
        V((1024, 16, 128), BF),
        V((2048, 128), F32),
        V((1024, 2048), BF),
        V((NC, 2048, W), F32),
        V((NC, 4, 4, 128, W), BF),
        V((NC, 4, 128, W), F32),
        V((128, 1024), BF),
        V((NC, 4, 2, 128, 128), BF),
        V((NC, 4, 2, 128, 128), BF),
        V((NC, 4, 128, W), BF),
        V((NC, 3, 128, W), BF),
        V((8, 8, 128), F32),
        V((7, 8, 128), F32),
        V((128, 1024), F32),
        V((NC, 8, W, 128), BF),
        V((NC, W, 128), F32),
        V((NC, 2, 3, 32, 16, 128), BF),
        V((NC, 2, 128, 128), F32),
        V((NC, 2, 3, 128, 128), BF),
        V((2048, W), BF),
        V((NC, 1024, W), BF),
        V((NC, 3, 256, W), BF),
        V((NC, 2, 3, 32, W), BF),
        V((NC, 3, 16, W), F32),
        V((NC, 256, W), F32),
        V((NC, 256, W), BF),
        V((NC, 64, W), F32),
    ]
    shapes = [
        (NC, 14), (7,), (NC,), (NC, 3), (NC, 4), (NC, 3), (NC, 12), (NC, 6), (NC, 2), (NC, 6),
        (NC, 6), (NC, 3),
    ]
    semaphores = [S((16,))] + [S(shape) for shape in shapes for _ in range(2)]
    results = pl.pallas_call(
        kernel,
        out_shape=(
            jax.ShapeDtypeStruct((128, 1024), BF),
            jax.ShapeDtypeStruct((16, 1024), F32),
        ),
        in_specs=[hbm] * 6 + [smem] * 2,
        out_specs=(vmem, vmem),
        scratch_shapes=buffers + semaphores,
        compiler_params=pltpu.CompilerParams(
            collective_id=0, has_side_effects=True, vmem_limit_bytes=63 * 1024 * 1024
        ),
        name="step",
    )(states, enc_weight, self_weight, neighbour_weight, edge_weight, out_grad, tile_live, overflow)
    return pl.pallas_call(
        hand_over,
        out_shape=tuple(jax.ShapeDtypeStruct(r.shape, r.dtype) for r in results),
        in_specs=[vmem] * 2,
        out_specs=(vmem,) * 2,
        name="hand_over",
    )(*results)


def solution(mesh):
    in_specs = (
        P(("text", "col"), None, None),
        P(),
        P(),
        P(),
        P("text", "col", None, None),
        P("text", "col", None),
        P(("text", "col"), None),
        P(),
    )
    out_specs = (P(("text", "col"), None), P(("text", "col"), None))
    return jax.shard_map(local, mesh=mesh, in_specs=in_specs, out_specs=out_specs, check_vma=False)
```

```python
import math

import jax
import jax.numpy as jnp
from jax import lax
from jax.experimental import pallas as pl
from jax.experimental.pallas import tpu as pltpu
from jax.sharding import PartitionSpec as P

MESH = pl.DeviceIdType.MESH
BF = jnp.bfloat16
F32 = jnp.float32
NC = 4
W = 256
STEPS = (1, 2, 3)


def dot(a, b):
    return jnp.dot(a, b, preferred_element_type=F32)


def dot_nt(a, b):
    return lax.dot_general(a, b, (((1,), (1,)), ((), ())), preferred_element_type=F32)


def kernel(
    states_h, enc_h, self_h, neigh_h, edge_h, grad_h, live, overflow,
    node_out, enc_grad,
    states, enc, w_self, w_neigh, edge, edge_f, adj, squash, feats, part, out_grad,
    core_out, core_in, zed_out, zed_in, deg_out, deg_in,
    pre, dagg, dself, hop1_in, keep, hop2_in, dzeta, rcore_in, rzed_in, rx_in, ry_in,
    sums, sums_out, last,
    load_sem, ag_s, ag_r, deg_s, deg_r, core_s, core_r, zed_s, zed_r, dg_s, dg_r, fw_s, fw_r,
    h1_s, h1_r, h2_s, h2_r, rc_s, rc_r, rz_s, rz_r, rx_s, rx_r, ry_s, ry_r,
):
    t = lax.axis_index("text")
    c = lax.axis_index("col")
    y, x, z, k = t // 4, t % 4, c // 2, c % 2
    other = 1 - k

    def at_x(d):
        return (y * 4 + (x + d) % 4, c)

    def at_y(d):
        return (((y + d) % 4) * 4 + x, c)

    def at_z(d):
        return (t, ((z + d) % 4) * 2 + k)

    def at_col(d):
        return (t, (c + d) % 8)

    sibling = (t, z * 2 + other)

    def describe(src, dst, ssem, rsem, to):
        return pltpu.make_async_remote_copy(
            src_ref=src, dst_ref=dst, send_sem=ssem, recv_sem=rsem, device_id=to,
            device_id_type=MESH,
        )

    def send(src, dst, ssem, rsem, to):
        copy = describe(src, dst, ssem, rsem, to)
        copy.start()
        return copy

    def load_states(m):
        rows = pl.ds(m * 512, 512)
        return pltpu.make_async_copy(states_h.at[rows], states.at[rows], load_sem.at[m])

    def load_enc(j):
        return pltpu.make_async_copy(enc_h.at[:, pl.ds(j * W, W)], enc.at[j], load_sem.at[8 + j])

    load_enc(0).start()
    load_states(0).start()
    rest = [
        pltpu.make_async_copy(src, dst, load_sem.at[12 + n])
        for n, (src, dst) in enumerate(
            [(edge_h, edge), (self_h, w_self), (neigh_h, w_neigh), (grad_h, out_grad)]
        )
    ]
    barrier = pltpu.get_barrier_semaphore()
    for d in STEPS:
        pl.semaphore_signal(barrier, inc=1, device_id=at_x(d), device_id_type=MESH)
        pl.semaphore_signal(barrier, inc=1, device_id=at_y(d), device_id_type=MESH)
    for d in range(1, 8):
        pl.semaphore_signal(barrier, inc=1, device_id=at_col(d), device_id_type=MESH)

    def encode(j):
        load_enc(j).wait()
        if j == 0:
            load_states(1).start()
        size = 512 if j == 0 else 1024

        def tile(m, _):
            rows = pl.ds(m * size, size)
            if j == 0:
                load_states(m).wait()

                @pl.when(m < 2)
                def _():
                    load_states(m + 2).start()

                @pl.when(m == 2)
                def _():
                    load_enc(1).start()

            s = jnp.tanh(dot(states[rows, :], enc[j]))
            squash[j, rows, :] = s
            mean = jnp.sum(s.reshape(size // 16, 16, W), axis=1) * (1.0 / 16.0)
            feats[j, y, x, pl.ds(m * (size // 16), size // 16), :] = mean.astype(BF)
            return 0

        lax.fori_loop(0, 2048 // size, tile, 0)

    LO, HI = pl.ds(0, 64), pl.ds(64, 64)

    def gather1(j):
        own_a, own_b = feats.at[j, y, x, LO], feats.at[j, y, x, HI]
        return [
            send(own_a, own_a, ag_s.at[j, d - 1], ag_r.at[j, d - 1], at_x(d)) for d in STEPS
        ] + [
            send(own_b, own_b, ag_s.at[j, 2 + d], ag_r.at[j, 2 + d], at_y(d)) for d in STEPS
        ]

    def gather2(j, first):
        for copy in first[:3]:
            copy.wait_recv()
        row = feats.at[j, y, :, LO]
        out = [
            send(row, row, ag_s.at[j, 6 + n], ag_r.at[j, 6 + n], at_y(d))
            for n, d in enumerate((1, 3))
        ]
        for copy in first[3:]:
            copy.wait_recv()
        column = feats.at[j, :, x, HI]
        return out + [
            send(column, column, ag_s.at[j, 8 + n], ag_r.at[j, 8 + n], at_x(d))
            for n, d in enumerate((1, 3))
        ]

    def gather3(j, second):
        out = []
        for n, d in enumerate((1, 3)):
            half = pl.ds(2 * n, 2)
            second[n].wait_recv()
            row = feats.at[j, (y + 4 - d) % 4, half, LO]
            out.append(send(row, row, ag_s.at[j, 10 + n], ag_r.at[j, 10 + n], at_y(d)))
            second[2 + n].wait_recv()
            column = feats.at[j, half, (x + 4 - d) % 4, HI]
            out.append(send(column, column, ag_s.at[j, 12 + n], ag_r.at[j, 12 + n], at_x(d)))
        return out

    def adjacency(r, _):
        rows = pl.ds(r * 128, 128)
        edge_f[...] = edge[rows].astype(F32).reshape(2048, 128)
        total = jnp.zeros((128, 128), F32)
        for i in range(16):
            a = edge_f[pl.ds(i, 128, stride=16), :] * live[r, i].astype(F32)
            adj[rows, i * 128 : (i + 1) * 128] = a.astype(BF)
            total = total + a
        column = jnp.broadcast_to(jnp.sum(total, axis=1, keepdims=True), (128, 128))
        deg_out[r] = column.T[0:8, :]
        return 0

    def aggregate(j, third):
        for copy in third:
            copy.wait_recv()
        p = dot(adj[...], feats[j].reshape(2048, W)).reshape(4, 2, 128, W)
        part[j] = jnp.where(k == 0, p[:, 0], p[:, 1])
        away = jnp.where(k == 0, p[:, 1], p[:, 0]).astype(BF)
        core_out[j, :, 0] = away[:, :, 0:128]
        core_out[j, :, 1] = away[:, :, 128:256]
        return send(core_out.at[j], core_in.at[j], core_s.at[j], core_r.at[j], sibling)

    def column_sum(j, copy):
        copy.wait_recv()
        for q in range(4):
            came = jnp.concatenate([core_in[j, q, 0], core_in[j, q, 1]], axis=1)
            total = part[j, q] + came.astype(F32)
            part[j, q] = total
            zed_out[j, q] = total.astype(BF)
        return [
            send(
                zed_out.at[j, (z + d) % 4], zed_in.at[j, d - 1],
                zed_s.at[j, d - 1], zed_r.at[j, d - 1], at_z(d),
            )
            for d in STEPS
        ]

    def combine(j, copies, scale):
        for copy in copies:
            copy.wait_recv()
        total = part[j, z]
        for d in range(3):
            total = total + zed_in[j, d].astype(F32)
        pooled = (total * scale).astype(BF)
        pre[...] += dot(pooled, w_neigh[pl.ds(j * W, W), :])

    encode(0)
    pl.semaphore_wait(barrier, 13)
    first, second, third = [gather1(0)], [], []
    for j in range(2, NC):
        load_enc(j).start()
    for copy in rest:
        copy.start()
    for j in range(1, NC):
        encode(j)
        first.append(gather1(j))
        second.append(gather2(j - 1, first[j - 1]))
    third.append(gather3(0, second[0]))
    rest[0].wait()
    lax.fori_loop(0, 4, adjacency, 0)
    second.append(gather2(NC - 1, first[NC - 1]))
    third.append(gather3(1, second[1]))
    lax.fori_loop(4, 8, adjacency, 0)
    deg_copies = [
        send(
            deg_out.at[(c + d) % 8], deg_in.at[d - 1], deg_s.at[d - 1], deg_r.at[d - 1], at_col(d)
        )
        for d in range(1, 8)
    ]
    def flip(m, _):
        def pair(n, _):
            a, b = pl.ds(m * 256, 256), pl.ds(n * 256, 256)
            up, down = states[a, b], states[b, a]
            states[a, b] = down.T
            states[b, a] = up.T
            return 0

        lax.fori_loop(0, m + 1, pair, 0)
        return 0

    core, zed = [aggregate(0, third[0])], []
    third.append(gather3(2, second[2]))
    third.append(gather3(3, second[3]))
    core.append(aggregate(1, third[1]))
    zed.append(column_sum(0, core[0]))
    core.append(aggregate(2, third[2]))
    zed.append(column_sum(1, core[1]))
    for copy in rest[1:]:
        copy.wait()
    own = jnp.concatenate([feats[j, y, x] for j in range(NC)], axis=1)
    pre[...] = dot(own, w_self[...])
    for copy in deg_copies:
        copy.wait_recv()
    degree = deg_out[c]
    for d in range(7):
        degree = degree + deg_in[d]
    inv_row = lax.rsqrt(1.0 + degree)[0:1, :]
    inv_column = jnp.broadcast_to(inv_row, (128, 128)).T[:, 0:1]
    combine(0, zed[0], inv_column)
    core.append(aggregate(3, third[3]))
    zed.append(column_sum(2, core[2]))
    combine(1, zed[1], inv_column)
    lax.fori_loop(0, 3, flip, 0)
    zed.append(column_sum(3, core[3]))
    combine(2, zed[2], inv_column)
    lax.fori_loop(3, 6, flip, 0)
    combine(3, zed[3], inv_column)

    v = pre[...]
    sg = 1.0 / (1.0 + jnp.exp(-v))
    node_out[...] = (v * sg).astype(BF)
    dpre = (out_grad[...].astype(F32) * sg * (1.0 + v * (1.0 - sg))).astype(BF)

    around = []

    def spread(j):
        dagg[j, c] = (dot_nt(w_neigh[pl.ds(j * W, W), :], dpre) * inv_row).astype(BF)
        own = dagg.at[j, c]
        around.append(
            [send(own, own, dg_s.at[j, d - 1], dg_r.at[j, d - 1], at_z(d)) for d in STEPS]
            + [send(own, own, dg_s.at[j, 3], dg_r.at[j, 3], sibling)]
        )

    spread(0)
    for j in range(NC):
        dself[j] = dot_nt(w_self[pl.ds(j * W, W), :], dpre)
    lax.fori_loop(6, 8, flip, 0)

    for copies in first + second + third + zed:
        for copy in copies:
            copy.wait_send()
    for copy in core + deg_copies:
        copy.wait_send()

    def forward(j):
        out = []
        for d in STEPS:
            around[j][d - 1].wait_recv()
            block = dagg.at[j, ((z - d + 4) % 4) * 2 + k]
            out.append(send(block, block, fw_s.at[j, d - 1], fw_r.at[j, d - 1], sibling))
        return out

    def piece(j, half, major, minor, blocks):
        return pl.ds(((j * 2 + half) * 16 + major * 4 + minor) * 8, blocks * 8)

    def transpose_product(j, passed):
        around[j][3].wait_recv()
        for copy in passed:
            copy.wait_recv()
        chunk = jnp.concatenate([dagg[j, q] for q in range(8)], axis=1)
        p = dot(chunk, adj[...]).astype(BF)
        for i in range(16):
            yy, xx, lanes = i // 4, i % 4, slice(i * 128, (i + 1) * 128)
            edge[piece(j, 0, yy, xx, 1)] = p[0:128, lanes].reshape(8, 16, 128)
            edge[piece(j, 1, xx, yy, 1)] = p[128:256, lanes].reshape(8, 16, 128)

    WAYS = ((1, 0, 2), (3, 2, 0))

    def scatter1(j):
        relayed, direct = [], []
        for n, (d, via, straight) in enumerate(WAYS):
            into = pl.ds(2 * n * 8, 16)
            for half, at, place in ((0, at_y, y), (1, at_x, x)):
                relayed.append(
                    send(
                        edge.at[piece(j, half, (place + 2) % 4, via, 2)],
                        hop1_in.at[j, half, 2, into],
                        h1_s.at[j, 2 * n + half], h1_r.at[j, 2 * n + half], at(d),
                    )
                )
        for n, (d, via, straight) in enumerate(WAYS):
            into = pl.ds(straight * 8, 16)
            for half, at, place in ((0, at_y, y), (1, at_x, x)):
                direct.append(
                    send(
                        edge.at[piece(j, half, (place + d) % 4, straight, 2)],
                        hop1_in.at[j, half, n, into],
                        h1_s.at[j, 4 + 2 * n + half], h1_r.at[j, 4 + 2 * n + half], at(d),
                    )
                )
        return relayed, direct

    def relay(j, relayed):
        out = []
        for n, (d, via, _) in enumerate(WAYS):
            for half, at, place in ((0, at_y, y), (1, at_x, x)):
                relayed[2 * n + half].wait_recv()
                mine = piece(j, half, (place + d) % 4, via, 2)
                came = hop1_in[j, half, 2, pl.ds(2 * n * 8, 16)].astype(F32)
                edge[mine] = (edge[mine].astype(F32) + came).astype(BF)
                out.append(
                    send(
                        edge.at[mine], hop1_in.at[j, half, n, pl.ds(via * 8, 16)],
                        h1_s.at[j, 8 + 2 * n + half], h1_r.at[j, 8 + 2 * n + half], at(d),
                    )
                )
        return out

    def scatter2(j, copies):
        for copy in copies:
            copy.wait_recv()
        for q in range(4):
            for half, place in ((0, y), (1, x)):
                total = edge[piece(j, half, place, q, 1)].astype(F32)
                for n in range(2):
                    total = total + hop1_in[j, half, n, pl.ds(q * 8, 8)].astype(F32)
                total = total.reshape(128, 128)
                part[0, q, :, half * 128 : half * 128 + 128] = total
                core_out[j, q, half] = total.astype(BF)
        keep[j, 0] = part[0, x, :, 0:128]
        keep[j, 1] = part[0, y, :, 128:256]
        out = []
        for d in STEPS:
            out.append(
                send(
                    core_out.at[j, (x + d) % 4, 0], hop2_in.at[j, 0, d - 1],
                    h2_s.at[j, d - 1], h2_r.at[j, d - 1], at_x(d),
                )
            )
            out.append(
                send(
                    core_out.at[j, (y + d) % 4, 1], hop2_in.at[j, 1, d - 1],
                    h2_s.at[j, 2 + d], h2_r.at[j, 2 + d], at_y(d),
                )
            )
        return out

    def encoder_term(j, copies):
        for copy in copies:
            copy.wait_recv()
        halves = []
        for h in range(2):
            total = keep[j, h]
            for d in range(3):
                total = total + hop2_in[j, h, d].astype(F32)
            halves.append(total)
        dx0 = jnp.concatenate(halves, axis=0) + dself[j]
        part[1, 0] = dx0.T * (1.0 / 16.0)

        def tile(m, _):
            rows = pl.ds(m * 256, 256)
            s = squash[j, rows, :].reshape(16, 16, W)
            g = part[1, 0, pl.ds(m * 16, 16), :].reshape(16, 1, W)
            dzeta[rows, :] = (g * (1.0 - s * s)).astype(BF).reshape(256, W)
            return 0

        lax.fori_loop(0, 8, tile, 0)

        def term(m, _):
            rows = pl.ds(m * 1024, 1024)
            squash[j, rows, :] = dot(states[rows, :], dzeta[...])
            for g in range(32):
                away = squash[j, pl.ds(m * 1024 + g * 32 + other * 16, 16), :].astype(BF)
                enc[j, pl.ds(m * 512 + g * 16, 16), :] = away
            raw_half(j, m).start()
            return 0

        lax.fori_loop(0, 2, term, 0)

    def raw_half(j, m):
        rows = pl.ds(m * 512, 512)
        return describe(
            enc.at[j, rows], rcore_in.at[j, rows], rc_s.at[j, m], rc_r.at[j, m], sibling
        )

    def term_zed(j, half):
        raw_half(j, half).wait_recv()
        base = 1024 + half * 512

        def tile(m, _):
            for q in range(4):
                g = m * 4 + q
                mine = pl.ds(g * 32 + k * 16, 16)
                total = squash[j, mine, :] + rcore_in[j, pl.ds(g * 16, 16), :].astype(F32)
                squash[j, mine, :] = total
                if half == 0:
                    slot = q * 128 + m * 16
                else:
                    slot = (m % 4) * 128 + ((m // 4 - 2) * 4 + q) * 16
                enc[j, pl.ds(base + slot, 16), :] = total.astype(BF)
            return 0

        lax.fori_loop(half * 8, half * 8 + 8, tile, 0)
        place, at = ((z, at_z), (x, at_x))[half]
        into = pl.ds(half * 128, 128)
        return [
            send(
                enc.at[j, pl.ds(base + ((place + d) % 4) * 128, 128)],
                rzed_in.at[j, d - 1, into],
                rz_s.at[j, half * 3 + d - 1], rz_r.at[j, half * 3 + d - 1], at(d),
            )
            for d in STEPS
        ]

    def term_x(j, half, copies):
        for copy in copies:
            copy.wait_recv()

        def tile(m, _):
            if half == 0:
                row = (m * 4 + z) * 32
                slot = (m % 4) * 32 + (m // 4) * 16
            else:
                row = (((2 + m // 4) * 4 + x) * 4 + m % 4) * 32
                slot = 128 + (m % 4) * 32 + (m // 4) * 16
            total = squash[j, pl.ds(row + k * 16, 16), :]
            for d in range(3):
                came = rzed_in[j, d, pl.ds(half * 128 + m * 16, 16), :]
                total = total + came.astype(F32)
            sums[j, pl.ds(slot, 16), :] = total
            sums_out[j, pl.ds(slot, 16), :] = total.astype(BF)
            return 0

        lax.fori_loop(0, 8, tile, 0)
        place, at = ((x, at_x), (z, at_z))[half]
        return [
            send(
                sums_out.at[j, pl.ds(half * 128 + ((place + d) % 4) * 32, 32)],
                rx_in.at[j, half, d - 1],
                rx_s.at[j, half * 3 + d - 1], rx_r.at[j, half * 3 + d - 1], at(d),
            )
            for d in STEPS
        ]

    def term_y(j, copies):
        for copy in copies:
            copy.wait_recv()
        for half, place in ((0, x), (1, z)):
            total = sums[j, pl.ds(half * 128 + place * 32, 32), :]
            for d in range(3):
                total = total + rx_in[j, half, d].astype(F32)
            last[j, half * 32 : half * 32 + 32, :] = total
        return [
            send(
                last.at[j, pl.ds(((y + d) % 4) * 16, 16)], ry_in.at[j, d - 1],
                ry_s.at[j, d - 1], ry_r.at[j, d - 1], at_y(d),
            )
            for d in STEPS
        ]

    factor = 1024.0 / (1024.0 + overflow[0].astype(F32)) * (16.0 / math.sqrt(16384 * 16))

    def finish(j, copies):
        for copy in copies:
            copy.wait_recv()
        total = last[j, pl.ds(y * 16, 16), :]
        for d in range(3):
            total = total + ry_in[j, d]
        enc_grad[:, j * W : (j + 1) * W] = total * factor

    passed, relayed, direct, hop1 = [], [], [], []
    hop2, rzed, rx, ry = [], [], [], []

    def product(j):
        passed.append(forward(j))
        if j + 1 < NC:
            spread(j + 1)
        transpose_product(j, passed[j])

    def first_hop(j):
        for kept, copies in zip((relayed, direct), scatter1(j)):
            kept.append(copies)

    def pass_on(j):
        hop1.append(relay(j, relayed[j]))

    def second_hop(j):
        hop2.append(scatter2(j, direct[j] + hop1[j]))

    def raw(j):
        encoder_term(j, hop2[j])

    def raw_z(j):
        rzed.append(term_zed(j, 0) + term_zed(j, 1))

    def raw_x(j):
        rx.append(term_x(j, 0, rzed[j][:3]) + term_x(j, 1, rzed[j][3:]))

    def raw_y(j):
        ry.append(term_y(j, rx[j]))

    for step, j in (
        (product, 0), (first_hop, 0), (product, 1), (pass_on, 0), (first_hop, 1), (product, 2),
        (pass_on, 1), (second_hop, 0), (first_hop, 2), (product, 3), (first_hop, 3),
        (second_hop, 1), (pass_on, 2), (raw, 0), (pass_on, 3), (second_hop, 2), (raw_z, 0),
        (raw, 1), (second_hop, 3), (raw_z, 1), (raw_x, 0), (raw, 2), (raw_z, 2), (raw_x, 1),
        (raw_y, 0), (raw, 3), (raw_z, 3), (raw_x, 2), (raw_y, 1), (raw_y, 2), (raw_x, 3),
        (raw_y, 3),
    ):
        step(j)
    for j in range(NC):
        finish(j, ry[j])

    for copies in around + passed + relayed + direct + hop1 + hop2 + rzed + rx + ry:
        for copy in copies:
            copy.wait_send()
    for j in range(NC):
        for half in range(2):
            raw_half(j, half).wait_send()


def hand_over(a, b, a_out, b_out):
    a_out[...] = a[...]
    b_out[...] = b[...]


def local(
    states, enc_weight, self_weight, neighbour_weight, edge_weight, tile_live, out_grad, overflow
):
    states = states.reshape(2048, 2048)
    edge_weight = edge_weight.reshape(1024, 16, 128)
    tile_live = tile_live.reshape(8, 16)
    hbm = pl.BlockSpec(memory_space=pl.ANY)
    smem = pl.BlockSpec(memory_space=pltpu.SMEM)
    vmem = pl.BlockSpec(memory_space=pltpu.VMEM)
    V, S = pltpu.VMEM, pltpu.SemaphoreType.DMA
    buffers = [
        V((2048, 2048), BF),
        V((NC, 2048, W), BF),
        V((1024, 1024), BF),
        V((1024, 1024), BF),
        V((1024, 16, 128), BF),
        V((2048, 128), F32),
        V((1024, 2048), BF),
        V((NC, 2048, W), F32),
        V((NC, 4, 4, 128, W), BF),
        V((NC, 4, 128, W), F32),
        V((128, 1024), BF),
        V((NC, 4, 2, 128, 128), BF),
        V((NC, 4, 2, 128, 128), BF),
        V((NC, 4, 128, W), BF),
        V((NC, 3, 128, W), BF),
        V((8, 8, 128), F32),
        V((7, 8, 128), F32),
        V((128, 1024), F32),
        V((NC, 8, W, 128), BF),
        V((NC, W, 128), F32),
        V((NC, 2, 3, 32, 16, 128), BF),
        V((NC, 2, 128, 128), F32),
        V((NC, 2, 3, 128, 128), BF),
        V((2048, W), BF),
        V((NC, 1024, W), BF),
        V((NC, 3, 256, W), BF),
        V((NC, 2, 3, 32, W), BF),
        V((NC, 3, 16, W), F32),
        V((NC, 256, W), F32),
        V((NC, 256, W), BF),
        V((NC, 64, W), F32),
    ]
    shapes = [
        (NC, 14), (7,), (NC,), (NC, 3), (NC, 4), (NC, 3), (NC, 12), (NC, 6), (NC, 2), (NC, 6),
        (NC, 6), (NC, 3),
    ]
    semaphores = [S((16,))] + [S(shape) for shape in shapes for _ in range(2)]
    results = pl.pallas_call(
        kernel,
        out_shape=(
            jax.ShapeDtypeStruct((128, 1024), BF),
            jax.ShapeDtypeStruct((16, 1024), F32),
        ),
        in_specs=[hbm] * 6 + [smem] * 2,
        out_specs=(vmem, vmem),
        scratch_shapes=buffers + semaphores,
        compiler_params=pltpu.CompilerParams(
            collective_id=0, has_side_effects=True, vmem_limit_bytes=63 * 1024 * 1024
        ),
        name="step",
    )(states, enc_weight, self_weight, neighbour_weight, edge_weight, out_grad, tile_live, overflow)
    return pl.pallas_call(
        hand_over,
        out_shape=tuple(jax.ShapeDtypeStruct(r.shape, r.dtype) for r in results),
        in_specs=[vmem] * 2,
        out_specs=(vmem,) * 2,
        name="hand_over",
    )(*results)


def solution(mesh):
    in_specs = (
        P(("text", "col"), None, None),
        P(),
        P(),
        P(),
        P("text", "col", None, None),
        P("text", "col", None),
        P(("text", "col"), None),
        P(),
    )
    out_specs = (P(("text", "col"), None), P(("text", "col"), None))
    return jax.shard_map(local, mesh=mesh, in_specs=in_specs, out_specs=out_specs, check_vma=False)
```
